512 devices in a mesh: seq: 32 (over z, x), head: 16 (over y, core).
Axes of the slice: x: 4, y: 8, z: 8, core: 2. Of those that a mesh axis runs over, the one named last changes fastest.
Arguments:
- projected: bfloat16 [65536, 3072], P(('seq', 'head')), may hold values from -28 to 28, as said below
- upstream: bfloat16 [65536, 768], P(('seq', 'head')), may hold values from -6 to 6
- out_weight: bfloat16 [768, 768], replicated, may hold values from -0.21875 to 0.21875
- tile_weights: bfloat16 [1536, 128, 128], P('seq'), may hold values from -0.5 to 0.5
- tile_owner: int32 [1536, 1], replicated, may hold values from 0 to 31; in each aligned block of 48 rows (0 to 47, 48 to 95, ...) at most 3 rows name the same one
- source_block: int32 [1536], replicated, may hold values from 0 to 15
- target_block: int32 [1536], replicated, may hold values from 0 to 15
- key_blocks: int32 [512, 4], P('seq'), may hold values from 0 to 15, as said below
- key_count: int32 [512], P('seq'), may hold values from 1 to 4, as said below
Outputs:
- layer_out: bfloat16 [65536, 768], P(('seq', 'head'))
- grad_projected: bfloat16 [65536, 3072], P(('seq', 'head'))
- weight_grad: float32 [768, 768], P('head', 'seq')
The draws below stay inside these ranges and needn't reach their ends.
Inputs may be any that keep to these rules, and one draw needn't show every extreme that they name: `projected`: queries and keys carry the scale of the score. `key_blocks`: row r lists distinct blocks, its own block r % 16 first. `key_count`: every shard has a query block that attends 4 key blocks. `tile_owner`: among the 48 tiles of one shard no owner is named more than 3 times, a bound that some block reaches.
All inputs are finite; a program needn't handle non-finite values.
Results may differ from the reference program's by a relative error of at most 0.0057.
Values may be sent and summed in bfloat16 or wider, within the bound.
A program may use at most 64 MiB of HBM per device.

```python
import math
import jax
import jax.numpy as jnp
import numpy as np
from jax import lax

D = 768
HEADS = 16
BLOCK = 128
CAP = 3
NODES = 65536
QB = 16
KMAX = 4
TILES = 48
TILES_ALL = 1536
N_SEQ = 32


def draw_projected(key, part):
    key = jax.random.fold_in(key, 11)
    head_size = D // HEADS
    subkeys = jax.random.split(key, 1)
    column_scale = jnp.array([1.5, 1.5, 1.0, 1.0], jnp.float32)[None, None, :, None]
    result = jax.random.truncated_normal(subkeys[0], -6.0, 6.0, (NODES, HEADS, 4, head_size), jnp.float32) * column_scale
    return result.reshape(NODES, HEADS * 4 * head_size).astype(jnp.bfloat16)


def draw_key_blocks(key, part):
    key = jax.random.fold_in(key, 12)
    row_total = N_SEQ * QB
    own_block = jnp.arange(row_total, dtype=jnp.int32) % QB
    subkeys = jax.random.split(key, row_total)
    shuffled = jax.vmap(lambda single: jax.random.permutation(single, QB - 1))(subkeys).astype(jnp.int32)
    others = (own_block[:, None] + 1 + shuffled[:, :KMAX - 1]) % QB
    return jnp.concatenate([own_block[:, None], others], axis=1).astype(jnp.int32)


def draw_key_count(key, part):
    key = jax.random.fold_in(key, 13)
    row_total = N_SEQ * QB
    subkeys = jax.random.split(key, 2)
    counts = jax.random.randint(subkeys[0], (row_total,), 1, KMAX + 1, dtype=jnp.int32)
    full_row = jax.random.randint(subkeys[1], (N_SEQ,), 0, QB, dtype=jnp.int32)
    is_full = jnp.arange(row_total, dtype=jnp.int32) % QB == jnp.repeat(full_row, QB)
    return jnp.where(is_full, KMAX, counts).astype(jnp.int32)


def touch_ends(entries, rng, smallest, high):
    extent = entries.shape
    spot = [jax.random.randint(jax.random.fold_in(rng, axis), (), 0, extent[axis]) for axis in range(len(extent))]
    entries = entries.at[tuple(spot)].set(smallest)
    longest = extent.index(max(extent))
    spot[longest] = (spot[longest] + 1) % extent[longest]
    return entries.at[tuple(spot)].set(high)


def level_of(key, dims, cuts, smallest, largest):
    def one(dim, blocks):
        draws = jax.random.uniform(jax.random.fold_in(jax.random.fold_in(key, 6), dim), (blocks,), jnp.float32, smallest / len(cuts), largest / len(cuts))
        return jnp.repeat(jnp.exp(draws), dims[dim] // blocks).reshape((-1,) + (1,) * (len(dims) - dim - 1))

    loudness = one(*cuts[0])
    for cut in cuts[1:]:
        loudness = loudness * one(*cut)
    return loudness


def shared_out(own_key, own, number, rows, number_of, top, bound, skew):
    sequence = jax.random.permutation(own_key, number_of)
    crowded, usual = portions_of(number_of, rows * top, bound, skew, True), portions_of(number_of, rows * top, bound, skew, False)
    places = jnp.arange(number_of)

    def named(sizes, turn):
        used = int((sizes > 0).sum())
        fixed = max(1, used // 4)
        shifted = fixed + (places - fixed + turn * (used - fixed)) % max(1, number_of - fixed)
        return jnp.zeros((number_of,), jnp.int32).at[sequence[jnp.where(places < fixed, places, shifted)]].set(jnp.asarray(sizes, jnp.int32))

    sizes = jnp.where(number % 4 == 0, named(crowded, number // 4), named(usual, number - number // 4 - 1))
    mixed = jax.random.permutation(jax.random.fold_in(own, 3), number_of)
    source_of, receiver = mixed[0:number_of // 2 * 2:2], mixed[1:number_of // 2 * 2:2]
    slack = jnp.minimum(sizes[source_of] - 1, bound - sizes[receiver]) // 2
    slack = jnp.where((source_of == sequence[0]) | (receiver == sequence[0]) | (sizes[receiver] == 0), 0, jnp.maximum(slack, 0))
    shifted = jax.random.randint(jax.random.fold_in(own, 4), (number_of // 2,), 0, 1 << 20) % (slack + 1)
    sizes = sizes.at[source_of].add(-shifted).at[receiver].add(shifted)
    items = jnp.searchsorted(jnp.cumsum(sizes), jnp.arange(rows * top), side="right").astype(jnp.int32)
    listing = items.reshape(top, rows).T
    listing = listing[jax.random.permutation(jax.random.fold_in(own, 1), rows)]
    turn = jax.random.randint(jax.random.fold_in(own, 2), (rows, 1), 0, top)
    return jnp.take_along_axis(listing, (jnp.arange(top)[None, :] + turn) % top, axis=1)


def portions_of(number_of, total, limit, skew, full):
    loads = [(1 << 20) // math.isqrt(rank ** skew) + 1 for rank in range(1, number_of + 1)]
    largest = limit if full else min(limit, max(-(-total // number_of), total * loads[0] // sum(loads)))
    least = 1 if total - largest >= number_of - 1 else 0
    holding, spare = [largest] + [least] * (number_of - 1), total - largest - least * (number_of - 1)
    while spare > 0:
        candidates = [i for i in range(1, number_of) if holding[i] < largest] or [i for i in range(1, number_of) if holding[i] < limit]
        mass, budget = sum([loads[i] for i in candidates]), spare
        for i in candidates:
            more = min(limit - holding[i], max(1, budget * loads[i] // mass), spare)
            holding[i] = holding[i] + more
            spare = spare - more
    return np.array(holding)


def normal_values(rng, dims, scale, bound, cuts=(), kind=jnp.bfloat16):
    loudness = level_of(rng, dims, cuts, -0.22, 0.18) if cuts else 1.0
    drawn = jax.random.normal(rng, dims, jnp.float32) * scale * loudness
    return jnp.minimum(jnp.maximum(drawn, -bound), bound).astype(kind)


def setup_inputs(seed: int = 0) -> dict:
    seeds = jax.random.split(jax.random.key(seed), 10)
    projected = draw_projected(jax.random.fold_in(seeds[9], 71), 0)
    upstream = normal_values(seeds[1], (NODES, D), 1.0, 6.0, ((0, 512),))
    out_weight = normal_values(seeds[2], (D, D), D ** -0.5, 0.21875)
    tile_weights = normal_values(seeds[3], (TILES_ALL, BLOCK, BLOCK), BLOCK ** -0.5, 0.5, ((0, 32),))
    tile_owner_keys = jax.random.split(jax.random.fold_in(seeds[4], 1), TILES_ALL // TILES)
    tile_owner_turns = jax.random.permutation(jax.random.fold_in(seeds[4], 3), TILES_ALL // TILES)
    tile_owner = jax.vmap(lambda own, number: shared_out(jax.random.fold_in(seeds[4], 2), own, number, TILES, N_SEQ, 1, CAP, 2))(tile_owner_keys, tile_owner_turns).reshape((TILES_ALL, 1))
    source_block = touch_ends(jax.random.randint(seeds[5], (TILES_ALL,), 0, QB), jax.random.fold_in(seeds[5], 1), 0, QB - 1).astype(jnp.int32)
    target_block = touch_ends(jax.random.randint(seeds[6], (TILES_ALL,), 0, QB), jax.random.fold_in(seeds[6], 1), 0, QB - 1).astype(jnp.int32)
    key_blocks = draw_key_blocks(jax.random.fold_in(seeds[9], 71), 0)
    key_count = draw_key_count(jax.random.fold_in(seeds[9], 71), 0)
    return dict(projected=projected, upstream=upstream, out_weight=out_weight, tile_weights=tile_weights, tile_owner=tile_owner, source_block=source_block, target_block=target_block, key_blocks=key_blocks, key_count=key_count)


def attend(query_rows, key_rows, value_rows, grad_rows, block_lists, block_counts):
    block_total, block_size, head_count, head_size = query_rows.shape
    slot_total = block_lists.shape[1]
    score_scale = head_size ** (-0.5)
    group_size = math.gcd(block_total, max(1, 512 // block_size))
    slot_ids = jnp.arange(slot_total, dtype=jnp.int32)
    usable_all = slot_ids[None, :] < block_counts[:, None]
    onehot_all = ((block_lists[:, :, None] == jnp.arange(block_total, dtype=jnp.int32)[None, None, :]) & usable_all[:, :, None]).astype(jnp.float32)

    def advance(running, step_index):
        acc_keys, acc_values = running
        first_block = step_index * group_size
        query_part = lax.dynamic_slice_in_dim(query_rows, first_block, group_size, 0).astype(jnp.float32)
        grad_part = lax.dynamic_slice_in_dim(grad_rows, first_block, group_size, 0).astype(jnp.float32)
        chosen = lax.dynamic_slice_in_dim(block_lists, first_block, group_size, 0)
        usable = lax.dynamic_slice_in_dim(usable_all, first_block, group_size, 0)
        onehot_part = lax.dynamic_slice_in_dim(onehot_all, first_block, group_size, 0)
        near_keys = key_rows[chosen].astype(jnp.float32)
        near_values = value_rows[chosen].astype(jnp.float32)
        scores = jnp.einsum('gihd,gjkhd->ghijk', query_part, near_keys) * score_scale
        scores = jnp.where(usable[:, None, None, :, None], scores, -jnp.inf)
        maximum = lax.optimization_barrier(jnp.max(scores, axis=(3, 4), keepdims=True))
        exponent = jnp.exp(scores - maximum)
        probability = exponent / lax.optimization_barrier(jnp.sum(exponent, axis=(3, 4), keepdims=True))
        probability_b = probability.astype(jnp.bfloat16)
        output = jnp.einsum('ghijk,gjkhd->gihd', probability_b.astype(jnp.float32), near_values).astype(jnp.bfloat16)
        grad_prob = jnp.einsum('gihd,gjkhd->ghijk', grad_part, near_values)
        row_delta = lax.optimization_barrier(jnp.sum(probability * grad_prob, axis=(3, 4), keepdims=True))
        dscore = (probability * (grad_prob - row_delta) * score_scale).astype(jnp.bfloat16).astype(jnp.float32)
        grad_query = jnp.einsum('ghijk,gjkhd->gihd', dscore, near_keys).astype(jnp.bfloat16)
        key_terms = jnp.einsum('ghijk,gihd->gjkhd', dscore, query_part)
        value_terms = jnp.einsum('ghijk,gihd->gjkhd', probability_b.astype(jnp.float32), grad_part)
        acc_keys = acc_keys + jnp.einsum('gjb,gjkhd->bkhd', onehot_part, key_terms, precision=lax.Precision.HIGHEST)
        acc_values = acc_values + jnp.einsum('gjb,gjkhd->bkhd', onehot_part, value_terms, precision=lax.Precision.HIGHEST)
        return ((acc_keys, acc_values), (output, grad_query))
    zero_grad = jnp.zeros(query_rows.shape, jnp.float32)
    (acc_keys, acc_values), (outputs, grad_queries) = lax.scan(advance, (zero_grad, zero_grad), jnp.arange(block_total // group_size, dtype=jnp.int32))
    return (outputs.reshape(query_rows.shape), grad_queries.reshape(query_rows.shape), acc_keys.astype(jnp.bfloat16), acc_values.astype(jnp.bfloat16))

def reference(projected, upstream, out_weight, tile_weights, tile_owner, source_block, target_block, key_blocks, key_count):
    head_size = D // HEADS
    viewed = projected.reshape(N_SEQ, QB, BLOCK, HEADS, 4, head_size)
    grad_attention = jnp.dot(upstream, out_weight.T, preferred_element_type=jnp.float32).astype(jnp.bfloat16)
    grad_heads = grad_attention.reshape(N_SEQ, QB, BLOCK, HEADS, head_size)
    block_lists = key_blocks.reshape(N_SEQ, QB, KMAX)
    block_counts = key_count.reshape(N_SEQ, QB)

    def one_shard(pieces):
        block_view, grad_view, list_view, count_view = pieces
        return attend(block_view[:, :, :, 0, :], block_view[:, :, :, 1, :], block_view[:, :, :, 2, :], grad_view, list_view, count_view)
    attended, grad_query, grad_key, grad_value = lax.map(one_shard, (viewed, grad_heads, block_lists, block_counts))
    features = viewed[:, :, :, :, 3, :].reshape(N_SEQ * QB, BLOCK, D)
    grad_blocks = upstream.reshape(N_SEQ * QB, BLOCK, D)
    owners = tile_owner[:, 0]
    shard_of = jnp.arange(N_SEQ * TILES, dtype=jnp.int32) // TILES
    source_global = (shard_of * QB + source_block).reshape(N_SEQ, TILES)
    target_global = owners * QB + target_block
    tiles_view = tile_weights.reshape(N_SEQ, TILES, BLOCK, BLOCK)

    def forward_tiles(pieces):
        weights_view, sources = pieces
        return jnp.einsum('tij,tjd->tid', weights_view.astype(jnp.float32), features[sources].astype(jnp.float32)).astype(jnp.bfloat16)
    partials = lax.map(forward_tiles, (tiles_view, source_global))
    mixed_sum = jax.ops.segment_sum(partials.reshape(N_SEQ * TILES, BLOCK * D).astype(jnp.float32), target_global, num_segments=N_SEQ * QB)
    mixed_nodes = mixed_sum.astype(jnp.bfloat16).reshape(NODES, D)

    def backward_tiles(pieces):
        weights_view, targets, sources = pieces
        tile_terms = jnp.einsum('tij,tid->tjd', weights_view.astype(jnp.float32), grad_blocks[targets].astype(jnp.float32))
        onehot = (sources[:, None] == jnp.arange(QB, dtype=jnp.int32)[None, :]).astype(jnp.float32)
        return jnp.einsum('tb,tjd->bjd', onehot, tile_terms, precision=lax.Precision.HIGHEST)
    grad_features = lax.map(backward_tiles, (tiles_view, target_global.reshape(N_SEQ, TILES), source_block.reshape(N_SEQ, TILES))).astype(jnp.bfloat16)
    attention_nodes = attended.reshape(NODES, D)
    layer_out = (jnp.dot(attention_nodes, out_weight, preferred_element_type=jnp.float32) + mixed_nodes.astype(jnp.float32)).astype(jnp.bfloat16)
    grad_projected = jnp.stack([grad_query, grad_key, grad_value, grad_features.reshape(N_SEQ, QB, BLOCK, HEADS, head_size)], axis=4).reshape(NODES, 4 * D)
    weight_grad = jnp.dot(attention_nodes.T, upstream, preferred_element_type=jnp.float32) * (1.0 / math.sqrt(NODES))
    return (layer_out, grad_projected, weight_grad)
```

```python
import functools
import math

import jax
import jax.numpy as jnp
from jax import lax
from jax.experimental import pallas as pl
from jax.experimental.pallas import tpu as pltpu
from jax.sharding import PartitionSpec as P

MESH = pl.DeviceIdType.MESH
HEADS = 16
BLOCK = 128
CAP = 3
HS = 48
D = 768
QB = 16
KMAX = 4
TILES = 48
SHARDS = 32
SLOTS = SHARDS * CAP
NX = 4
NZ = 8
F32 = jnp.float32
BF16 = jnp.bfloat16

T_TILE_OF = 0
T_SRC = T_TILE_OF + SLOTS
T_SLOT_OF = T_SRC + TILES
T_PREV_SRC = T_SLOT_OF + TILES
T_LAST_SRC = T_PREV_SRC + TILES
T_REPLY = T_LAST_SRC + QB
T_PREV_TGT = T_REPLY + SLOTS
T_LAST_TGT = T_PREV_TGT + SLOTS
T_KEY = T_LAST_TGT + QB
T_COUNT = T_KEY + QB * KMAX
T_PREV_KEY = T_COUNT + QB
T_LAST_KEY = T_PREV_KEY + QB * KMAX
T_ALL = T_LAST_KEY + QB


def nn(a, b):
    return lax.dot_general(a, b, (((1,), (0,)), ((), ())), preferred_element_type=F32)


def nt(a, b):
    return lax.dot_general(a, b, (((1,), (1,)), ((), ())), preferred_element_type=F32)


def each(start, stop, unroll=1):
    def run(f):
        def step(i, carry):
            f(i)
            return carry

        lax.fori_loop(start, stop, step, 0, unroll=unroll)

    return run


def kernel(
    tab, pj, up, ow, tw,
    lo_out, gp_out, wg_out,
    pjv, upv, owv, twv,
    p_f, p_q, f_t, q_t, u_t, g_t, kv,
    part, outg, arr, rep, retd,
    run_t, run_s, run_k, run_v,
    s_a, s_kv, s_f, s_m, r_a, r_kv, r_f, r_m,
    wg_acc, wg_p, wx_r, wz_p, wz_r,
    ld, fs, fr, qs, qr, rs, rr, ls, lr, bs, br, ps, pr, es, er,
    as_, ar, ks, kr, hs, hr, ms, mr, xs, xr, zs, zr,
):
    s = lax.axis_index("seq")
    h = lax.axis_index("head")
    z = s // NX
    x = s % NX
    sib = h + 1 - 2 * (h % 2)
    right, left = (h + 2) % HEADS, (h + HEADS - 2) % HEADS
    my_rows = pl.ds(pl.multiple_of(h * HS, 16), HS)

    def remote(src, dst, send, recv, axis, peer):
        return pltpu.make_async_remote_copy(
            src_ref=src, dst_ref=dst, send_sem=send, recv_sem=recv,
            device_id={axis: peer}, device_id_type=MESH,
        )

    def head_copy(src, dst, send, recv):
        def at(d):
            peer = (h + d) % HEADS
            return remote(src.at[peer], dst.at[h], send.at[d], recv.at[d], "head", peer)

        return at

    def seq_copy(src, dst, send, recv):
        def at(d):
            peer = (s + d) % SHARDS
            return remote(
                src.at[pl.ds(peer * CAP, CAP)], dst.at[pl.ds(s * CAP, CAP)],
                send.at[d], recv.at[d], "seq", peer,
            )

        return at

    c_f = head_copy(p_f, f_t, fs, fr)
    c_q = head_copy(p_q, q_t, qs, qr)
    c_a = head_copy(s_a, r_a, as_, ar)
    c_kv = head_copy(s_kv, r_kv, ks, kr)
    c_df = head_copy(s_f, r_f, hs, hr)
    c_m = head_copy(s_m, r_m, ms, mr)
    c_p = seq_copy(outg, arr, ps, pr)
    c_e = seq_copy(rep, retd, es, er)

    def start_all(copy, n):
        each(1, n)(lambda d: copy(d).start())

    def recv_all(copy, n):
        each(1, n)(lambda d: copy(d).wait_recv())

    def send_all(copy, n):
        each(1, n)(lambda d: copy(d).wait_send())

    half = D // 2
    parts_right = [pl.ds(0, D)] * 3 + [pl.ds(0, half)]
    parts_left = [pl.ds(0, D)] * 3 + [pl.ds(half, half)]

    def ring_right(i):
        ref = u_t.at[(h + HEADS - 2 * i) % HEADS, parts_right[i]]
        return remote(ref, ref, rs.at[i], rr.at[i], "head", right)

    def ring_left(i):
        ref = u_t.at[(h + 2 * i) % HEADS, parts_left[i]]
        return remote(ref, ref, ls.at[i], lr.at[i], "head", left)

    def to_sib(k):
        ref = u_t.at[(h + 2 * k) % HEADS]
        return remote(ref, ref, bs.at[k], br.at[k], "head", sib)

    l_up = pltpu.make_async_copy(up, upv, ld.at[0])
    l_pj = pltpu.make_async_copy(pj, pjv, ld.at[1])
    l_tw = pltpu.make_async_copy(tw, twv, ld.at[2])
    l_ow = pltpu.make_async_copy(ow, owv, ld.at[3])
    for load in (l_up, l_pj, l_tw, l_ow):
        load.start()
    barrier = pltpu.get_barrier_semaphore()

    @each(1, HEADS)
    def _(d):
        pl.semaphore_signal(
            barrier, inc=1, device_id={"head": (h + d) % HEADS}, device_id_type=MESH
        )

    @each(1, SHARDS)
    def _(d):
        pl.semaphore_signal(
            barrier, inc=1, device_id={"seq": (s + d) % SHARDS}, device_id_type=MESH
        )

    run_t[SLOTS] = jnp.zeros((HS, BLOCK), F32)
    run_s[TILES] = jnp.zeros((HS, BLOCK), F32)
    run_k[QB * KMAX] = jnp.zeros((HS, BLOCK), F32)
    run_v[QB * KMAX] = jnp.zeros((HS, BLOCK), F32)

    l_up.wait()
    for i in range(2):
        u_t[h, half * i : half * (i + 1)] = upv[:, half * i : half * (i + 1)].T
    l_pj.wait()
    for i in range(HEADS // 2):
        pair = pjv[:, 8 * HS * i : 8 * HS * (i + 1)].T
        for k in range(2):
            p_q[2 * i + k] = pair[4 * HS * k : 4 * HS * k + 3 * HS]
            p_f[2 * i + k] = pair[4 * HS * k + 3 * HS : 4 * HS * (k + 1)]
    f_t[h] = p_f[h]
    q_t[h] = p_q[h]
    pl.semaphore_wait(barrier, HEADS + SHARDS - 2)

    start_all(c_f, HEADS)
    ring_right(0).start()
    ring_left(0).start()
    to_sib(0).start()
    start_all(c_q, HEADS)

    def ring_step(i):
        ring_right(i - 1).wait_recv()
        if i < 4:
            ring_right(i).start()
            to_sib(8 - i).start()
        ring_left(i - 1).wait_recv()
        if i < 4:
            ring_left(i).start()
            to_sib(i).start()
        else:
            to_sib(4).start()

    recv_all(c_f, HEADS)
    l_tw.wait()

    @each(0, TILES, 8)
    def _(t):
        part[t] = nt(f_t[tab[T_SRC + t]], twv[t]).astype(BF16)

    @each(0, SLOTS, 8)
    def _(p):
        outg[p] = part[tab[T_TILE_OF + p]]

    start_all(c_p, SHARDS)
    arr[pl.ds(s * CAP, CAP)] = outg[pl.ds(s * CAP, CAP)]
    ring_step(1)
    ring_step(2)
    ring_step(3)
    ring_step(4)
    each(0, 8)(lambda k: to_sib(k).wait_recv())

    @each(0, SLOTS, 8)
    def _(p):
        rep[p] = u_t[tab[T_REPLY + p], my_rows]

    start_all(c_e, SHARDS)
    retd[pl.ds(s * CAP, CAP)] = rep[pl.ds(s * CAP, CAP)]

    l_ow.wait()

    @each(0, QB, 2)
    def _(b):
        g_t[b] = nn(owv[my_rows], u_t[b]).astype(BF16)

    recv_all(c_q, HEADS)

    @each(0, QB, 2)
    def _(b):
        kv[b] = q_t[b, HS:].T

    scale = HS ** (-0.5)
    pad = jnp.zeros((HS, BLOCK), BF16)

    def attend(i):
        r = (h + 1 + i) % QB
        q = q_t[r, :HS]
        g = g_t[r]
        blocks = [tab[T_KEY + KMAX * i + j] for j in range(KMAX)]
        count = tab[T_COUNT + i]
        qg = jnp.concatenate(
            [jnp.concatenate([q, pad], axis=1), jnp.concatenate([pad, g], axis=1)], axis=0
        )
        both = [nn(kv[blocks[j]], qg) for j in range(KMAX)]
        scores = [
            both[j][:, :BLOCK] * scale + jnp.where(j < count, 0.0, -jnp.inf).astype(F32)
            for j in range(KMAX)
        ]
        grad_prob = [both[j][:, BLOCK:] for j in range(KMAX)]
        top = functools.reduce(
            jnp.maximum, [jnp.max(sc, axis=0, keepdims=True) for sc in scores]
        )
        expo = [jnp.exp(sc - top) for sc in scores]
        total = sum(jnp.sum(e, axis=0, keepdims=True) for e in expo)
        inverse = 1.0 / total
        prob = [e * inverse for e in expo]
        delta = sum(
            jnp.sum(a * b, axis=0, keepdims=True) for a, b in zip(prob, grad_prob)
        )
        prob_b = jnp.concatenate([a.astype(BF16) for a in prob], axis=0)
        dscore = jnp.concatenate(
            [(a * (b - delta) * scale).astype(BF16) for a, b in zip(prob, grad_prob)], axis=0
        )
        keys_t = jnp.concatenate([q_t[b, HS : 2 * HS] for b in blocks], axis=1)
        values_t = jnp.concatenate([q_t[b, 2 * HS :] for b in blocks], axis=1)
        s_a[r, :HS] = nn(values_t, prob_b).astype(BF16)
        s_a[r, HS:] = nn(keys_t, dscore).astype(BF16)
        term_k = nt(q, dscore)
        term_v = nt(g, prob_b)
        for j in range(KMAX):
            before = tab[T_PREV_KEY + KMAX * i + j]
            lanes = slice(BLOCK * j, BLOCK * (j + 1))
            run_k[KMAX * i + j] = term_k[:, lanes] + run_k[before]
            run_v[KMAX * i + j] = term_v[:, lanes] + run_v[before]

    @each(0, QB - 1)
    def _(i):
        attend(i)
        c_a(i + 1).start()

    attend(QB - 1)
    r_a[h] = s_a[h]

    @each(1, HEADS)
    def _(d):
        b = (h + d) % HEADS
        last = tab[T_LAST_KEY + b]
        s_kv[b, :HS] = run_k[last].astype(BF16)
        s_kv[b, HS:] = run_v[last].astype(BF16)
        c_kv(d).start()

    last_own = tab[T_LAST_KEY + h]
    r_kv[h, :HS] = run_k[last_own].astype(BF16)
    r_kv[h, HS:] = run_v[last_own].astype(BF16)

    wg_acc[...] = nt(u_t[0], s_a[0, :HS])

    @each(1, QB)
    def _(b):
        wg_acc[...] += nt(u_t[b], s_a[b, :HS])

    columns = D // SHARDS
    for n in range(SHARDS):
        wg_p[(n % NX) * NZ + n // NX] = wg_acc[columns * n : columns * (n + 1)]

    def c_x(d):
        to = (x + d) % NX
        return remote(
            wg_p.at[pl.ds(to * NZ, NZ)], wx_r.at[x], xs.at[d], xr.at[d], "seq", z * NX + to
        )

    def c_z(d):
        to = (z + d) % NZ
        return remote(wz_p.at[to], wz_r.at[z], zs.at[d], zr.at[d], "seq", to * NX + x)

    start_all(c_x, NX)
    wx_r[x] = wg_p[pl.ds(x * NZ, NZ)]

    recv_all(c_p, SHARDS)

    @each(0, SLOTS, 8)
    def _(p):
        run_t[p] = arr[p].astype(F32) + run_t[tab[T_PREV_TGT + p]]

    @each(1, HEADS)
    def _(d):
        b = (h + d) % HEADS
        s_m[b] = run_t[tab[T_LAST_TGT + b]].astype(BF16)
        c_m(d).start()

    r_m[h] = run_t[tab[T_LAST_TGT + h]].astype(BF16)

    recv_all(c_x, NX)
    wz_p[...] = wx_r[0] + wx_r[1] + wx_r[2] + wx_r[3]
    start_all(c_z, NZ)
    wz_r[z] = wz_p[z]

    recv_all(c_e, SHARDS)

    @each(0, TILES, 8)
    def _(t):
        run_s[t] = nn(retd[tab[T_SLOT_OF + t]], twv[t])

    @each(0, TILES, 8)
    def _(t):
        run_s[t] = run_s[t] + run_s[tab[T_PREV_SRC + t]]

    @each(1, HEADS)
    def _(d):
        b = (h + d) % HEADS
        s_f[b] = run_s[tab[T_LAST_SRC + b]].astype(BF16)
        c_df(d).start()

    r_f[h] = run_s[tab[T_LAST_SRC + h]].astype(BF16)

    recv_all(c_z, NZ)
    total = wz_r[0]
    for n in range(1, NZ):
        total = total + wz_r[n]
    wg_out[...] = (total * (1.0 / math.sqrt(SHARDS * QB * BLOCK))).T

    recv_all(c_a, HEADS)
    recv_all(c_m, HEADS)
    per = HEADS // 2
    acc = jnp.zeros((BLOCK, D), F32)
    for i in range(2):
        wide = jnp.concatenate([r_a[per * i + k, :HS] for k in range(per)], axis=0).T
        acc = acc + nn(wide, owv[half * i : half * (i + 1)])
    mixed = [
        jnp.concatenate([r_m[per * i + k] for k in range(per)], axis=0).T for i in range(2)
    ]
    lo_out[...] = (acc + jnp.concatenate(mixed, axis=1).astype(F32)).astype(BF16)
    recv_all(c_kv, HEADS)
    recv_all(c_df, HEADS)
    for i in range(HEADS // 2):
        rows = []
        for n in (2 * i, 2 * i + 1):
            rows += [r_a[n, HS:], r_kv[n], r_f[n]]
        gp_out[:, 8 * HS * i : 8 * HS * (i + 1)] = jnp.concatenate(rows, axis=0).T

    for copy in (c_f, c_q, c_a, c_kv, c_df, c_m):
        send_all(copy, HEADS)
    send_all(c_p, SHARDS)
    send_all(c_e, SHARDS)
    send_all(c_x, NX)
    send_all(c_z, NZ)
    for i in range(4):
        ring_right(i).wait_send()
        ring_left(i).wait_send()
    each(0, 8)(lambda k: to_sib(k).wait_send())


def last_before(same):
    n = same.shape[-1]
    return jnp.max(jnp.where(same, jnp.arange(n, dtype=jnp.int32), -1), axis=-1)


def earlier(n):
    r = jnp.arange(n, dtype=jnp.int32)
    return r[None, :] < r[:, None]


def tables(tile_owner, source_block, target_block, key_blocks, key_count):
    s = lax.axis_index("seq")
    h = lax.axis_index("head")
    blocks = jnp.arange(QB, dtype=jnp.int32)
    owners = tile_owner.reshape(SHARDS, TILES)
    targets = target_block.reshape(SHARDS, TILES)
    mine = lax.dynamic_index_in_dim(owners, s, 0, keepdims=False)
    src = lax.dynamic_slice_in_dim(source_block, s * TILES, TILES, 0)

    def chained(labels, none):
        prev = last_before((labels[:, None] == labels[None, :]) & earlier(labels.shape[0]))
        last = last_before(blocks[:, None] == labels[None, :])
        return jnp.where(prev < 0, none, prev), jnp.where(last < 0, none, last)

    rank = jnp.sum(((mine[:, None] == mine[None, :]) & earlier(TILES)).astype(jnp.int32), axis=1)
    slot_of = mine * CAP + rank
    slots = jnp.arange(SLOTS, dtype=jnp.int32)
    tile_of = jnp.maximum(last_before(slots[:, None] == slot_of[None, :]), 0)
    prev_src, last_src = chained(src, TILES)
    to_me = owners == s
    rank_in = jnp.sum((to_me[:, None, :] & earlier(TILES)[None]).astype(jnp.int32), axis=2)
    held = to_me[:, None, :] & (
        rank_in[:, None, :] == jnp.arange(CAP, dtype=jnp.int32)[None, :, None]
    )
    target = jnp.max(jnp.where(held, targets[:, None, :], -1), axis=2).reshape(SLOTS)
    prev_tgt, last_tgt = chained(target, SLOTS)
    order = (h + 1 + blocks) % QB
    keys = key_blocks[order].reshape(QB * KMAX)
    prev_key, last_key = chained(keys, QB * KMAX)
    return jnp.concatenate(
        [
            tile_of, src, slot_of, prev_src, last_src, jnp.maximum(target, 0), prev_tgt, last_tgt,
            keys, key_count[order], prev_key, last_key,
        ]
    )


def body(
    projected, upstream, out_weight, tile_weights, tile_owner,
    source_block, target_block, key_blocks, key_count,
):
    tab = tables(tile_owner, source_block, target_block, key_blocks, key_count)
    any_space = pl.BlockSpec(memory_space=pl.ANY)
    vmem = pl.BlockSpec(memory_space=pltpu.VMEM)

    def buf(*shape, dtype=BF16):
        return pltpu.VMEM(shape, dtype)

    def sems(n):
        return pltpu.SemaphoreType.DMA((n,))

    tiles = (HS, BLOCK)
    return pl.pallas_call(
        kernel,
        out_shape=(
            jax.ShapeDtypeStruct((BLOCK, D), BF16),
            jax.ShapeDtypeStruct((BLOCK, 4 * D), BF16),
            jax.ShapeDtypeStruct((HS, D // SHARDS), F32),
        ),
        in_specs=[pl.BlockSpec(memory_space=pltpu.SMEM)] + [any_space] * 4,
        out_specs=(vmem, vmem, vmem),
        scratch_shapes=[
            buf(BLOCK, 4 * D), buf(BLOCK, D), buf(D, D), buf(TILES, BLOCK, BLOCK),
            buf(HEADS, *tiles), buf(HEADS, 3 * HS, BLOCK),
            buf(HEADS, *tiles), buf(HEADS, 3 * HS, BLOCK),
            buf(QB, D, BLOCK), buf(QB, *tiles), buf(QB, BLOCK, 2 * HS),
            buf(TILES, *tiles), buf(SLOTS, *tiles), buf(SLOTS, *tiles),
            buf(SLOTS, *tiles), buf(SLOTS, *tiles),
            buf(SLOTS + 1, *tiles, dtype=F32), buf(TILES + 1, *tiles, dtype=F32),
            buf(QB * KMAX + 1, *tiles, dtype=F32), buf(QB * KMAX + 1, *tiles, dtype=F32),
            buf(HEADS, 2 * HS, BLOCK), buf(HEADS, 2 * HS, BLOCK),
            buf(HEADS, *tiles), buf(HEADS, *tiles),
            buf(HEADS, 2 * HS, BLOCK), buf(HEADS, 2 * HS, BLOCK),
            buf(HEADS, *tiles), buf(HEADS, *tiles),
            buf(D, HS, dtype=F32), buf(SHARDS, D // SHARDS, HS, dtype=F32),
            buf(NX, NZ, D // SHARDS, HS, dtype=F32),
            buf(NZ, D // SHARDS, HS, dtype=F32), buf(NZ, D // SHARDS, HS, dtype=F32),
            sems(4), sems(HEADS), sems(HEADS), sems(HEADS), sems(HEADS),
            sems(4), sems(4), sems(4), sems(4), sems(8), sems(8),
            sems(SHARDS), sems(SHARDS), sems(SHARDS), sems(SHARDS),
            sems(HEADS), sems(HEADS), sems(HEADS), sems(HEADS),
            sems(HEADS), sems(HEADS), sems(HEADS), sems(HEADS),
            sems(NX), sems(NX), sems(NZ), sems(NZ),
        ],
        compiler_params=pltpu.CompilerParams(
            collective_id=0, has_side_effects=True, vmem_limit_bytes=48 << 20
        ),
    )(tab, projected, upstream, out_weight, tile_weights)


def solution(mesh):
    in_specs = (
        P(("seq", "head"), None), P(("seq", "head"), None), P(), P("seq", None, None),
        P(), P(), P(), P("seq", None), P("seq"),
    )
    out_specs = (P(("seq", "head"), None), P(("seq", "head"), None), P("head", "seq"))
    return jax.shard_map(body, mesh=mesh, in_specs=in_specs, out_specs=out_specs, check_vma=False)
```

```python
import functools
import math

import jax
import jax.numpy as jnp
from jax import lax
from jax.experimental import pallas as pl
from jax.experimental.pallas import tpu as pltpu
from jax.sharding import PartitionSpec as P

MESH = pl.DeviceIdType.MESH
HEADS = 16
BLOCK = 128
CAP = 3
HS = 48
D = 768
QB = 16
KMAX = 4
TILES = 48
SHARDS = 32
SLOTS = SHARDS * CAP
NX = 4
NZ = 8
F32 = jnp.float32
BF16 = jnp.bfloat16

SLOT_OF, PREV_SRC, LAST_SRC, PREV_TGT, LAST_TGT, PREV_KEY, LAST_KEY = range(7)


def nn(a, b):
    return lax.dot_general(a, b, (((1,), (0,)), ((), ())), preferred_element_type=F32)


def nt(a, b):
    return lax.dot_general(a, b, (((1,), (1,)), ((), ())), preferred_element_type=F32)


def each(start, stop, unroll=1):
    def run(f):
        def step(i, carry):
            f(i)
            return carry

        lax.fori_loop(start, stop, step, 0, unroll=unroll)

    return run


def kernel(
    own_in, sources_in, targets_in, keys_in, counts_in, pj, up, ow, tw,
    lo_out, q_out, r_kv, r_f, wg_out,
    own, sources, targets, keys, counts, lo_v, wg_v,
    own_m, slots_v, slots, chains_v, chains,
    pjv, upv, owv, twv,
    p_f, p_q, f_t, q_t, u_t, g_t, kv,
    part, outg, arr, rep, retd,
    run_t, run_s, run_k, run_v,
    s_a, s_kv, s_f, s_m, r_a, r_m,
    wg_acc, wg_p, wx_r, wz_p, wz_r,
    ld, tb, out, fs, fr, qs, qr, rs, rr, ls, lr, bs, br, ps, pr, es, er,
    as_, ar, ks, kr, hs, hr, ms, mr, xs, xr, zs, zr,
):
    s = lax.axis_index("seq")
    h = lax.axis_index("head")
    z = s // NX
    x = s % NX
    sib = h + 1 - 2 * (h % 2)
    right, left = (h + 2) % HEADS, (h + HEADS - 2) % HEADS
    my_rows = pl.ds(pl.multiple_of(h * HS, 16), HS)

    def remote(src, dst, send, recv, axis, peer):
        return pltpu.make_async_remote_copy(
            src_ref=src, dst_ref=dst, send_sem=send, recv_sem=recv,
            device_id={axis: peer}, device_id_type=MESH,
        )

    def head_copy(src, dst, send, recv):
        def at(d):
            peer = (h + d) % HEADS
            return remote(src.at[peer], dst.at[h], send.at[d], recv.at[d], "head", peer)

        return at

    def seq_copy(src, dst, send, recv):
        def at(d):
            peer = (s + d) % SHARDS
            return remote(
                src.at[pl.ds(peer * CAP, CAP)], dst.at[pl.ds(s * CAP, CAP)],
                send.at[d], recv.at[d], "seq", peer,
            )

        return at

    c_f = head_copy(p_f, f_t, fs, fr)
    c_q = head_copy(p_q, q_t, qs, qr)
    c_a = head_copy(s_a, r_a, as_, ar)
    c_kv = head_copy(s_kv, r_kv, ks, kr)
    c_df = head_copy(s_f, r_f, hs, hr)
    c_m = head_copy(s_m, r_m, ms, mr)
    c_p = seq_copy(outg, arr, ps, pr)
    c_e = seq_copy(rep, retd, es, er)

    def start_all(copy, n):
        each(1, n)(lambda d: copy(d).start())

    def recv_all(copy, n):
        each(1, n)(lambda d: copy(d).wait_recv())

    def send_all(copy, n):
        each(1, n)(lambda d: copy(d).wait_send())

    half = D // 2
    parts_right = [pl.ds(0, D)] * 3 + [pl.ds(0, half)]
    parts_left = [pl.ds(0, D)] * 3 + [pl.ds(half, half)]

    def ring_right(i):
        ref = u_t.at[(h + HEADS - 2 * i) % HEADS, parts_right[i]]
        return remote(ref, ref, rs.at[i], rr.at[i], "head", right)

    def ring_left(i):
        ref = u_t.at[(h + 2 * i) % HEADS, parts_left[i]]
        return remote(ref, ref, ls.at[i], lr.at[i], "head", left)

    def to_sib(k):
        ref = u_t.at[(h + 2 * k) % HEADS]
        return remote(ref, ref, bs.at[k], br.at[k], "head", sib)

    l_up = pltpu.make_async_copy(up, upv, ld.at[0])
    l_pj = pltpu.make_async_copy(pj, pjv, ld.at[1])
    l_tw = pltpu.make_async_copy(tw, twv, ld.at[2])
    l_ow = pltpu.make_async_copy(ow, owv, ld.at[3])
    small = (
        (own_in, own), (sources_in, sources), (targets_in, targets), (keys_in, keys),
        (counts_in, counts),
    )
    l_small = [pltpu.make_async_copy(a, b, ld.at[4 + n]) for n, (a, b) in enumerate(small)]
    l_pj.start()
    l_up.start()
    barrier = pltpu.get_barrier_semaphore()
    for d in range(1, HEADS):
        pl.semaphore_signal(
            barrier, inc=1, device_id={"head": (h + d) % HEADS}, device_id_type=MESH
        )
    for d in range(1, SHARDS):
        pl.semaphore_signal(
            barrier, inc=1, device_id={"seq": (s + d) % SHARDS}, device_id_type=MESH
        )
    for load in (*l_small, l_tw, l_ow):
        load.start()
    l_pj.wait()
    for i in range(HEADS // 2):
        pair = pjv[:, 8 * HS * i : 8 * HS * (i + 1)].T
        for k in range(2):
            p_q[2 * i + k] = pair[4 * HS * k : 4 * HS * k + 3 * HS]
            p_f[2 * i + k] = pair[4 * HS * k + 3 * HS : 4 * HS * (k + 1)]
    pl.semaphore_wait(barrier, HEADS + SHARDS - 2)

    start_all(c_f, HEADS)
    f_t[h] = p_f[h]
    q_t[h] = p_q[h]
    l_up.wait()
    for i in range(2):
        u_t[h, half * i : half * (i + 1)] = upv[:, half * i : half * (i + 1)].T
    run_t[SLOTS] = jnp.zeros((HS, BLOCK), F32)
    run_s[TILES] = jnp.zeros((HS, BLOCK), F32)
    run_k[QB * KMAX] = jnp.zeros((HS, BLOCK), F32)
    run_v[QB * KMAX] = jnp.zeros((HS, BLOCK), F32)

    def ring_step(i):
        ring_right(i - 1).wait_recv()
        if i < 4:
            ring_right(i).start()
            to_sib(8 - i).start()
        ring_left(i - 1).wait_recv()
        if i < 4:
            ring_left(i).start()
            to_sib(i).start()
        else:
            to_sib(4).start()

    for load in l_small:
        load.wait()
    for n in range(SHARDS):
        own_m[n : n + 1, :TILES] = own[:, TILES * n : TILES * (n + 1)]
    lane = lax.broadcasted_iota(jnp.int32, (SHARDS, BLOCK), 1)
    row = lax.broadcasted_iota(jnp.int32, (SHARDS, BLOCK), 0)
    lane1 = lax.broadcasted_iota(jnp.int32, (1, BLOCK), 1)

    def first_three(same):
        found = []
        for k in range(CAP):
            later = same & (lane > found[-1]) if k else same
            found.append(jnp.min(jnp.where(later, lane, 999), axis=1, keepdims=True))
        return found

    def in_lanes(found, none):
        listed = jnp.where(lane == 0, found[0], jnp.where(lane == 1, found[1], found[2]))
        return jnp.where(listed == 999, none, listed)

    mine = own_m[pl.ds(s, 1), :]
    going = first_three((mine == row) & (lane < TILES))
    coming = first_three((own_m[...] == s) & (lane < TILES))
    slots_v[:SHARDS] = in_lanes(going, 0)
    slots_v[SHARDS:] = in_lanes(coming, -1)
    l_slots = pltpu.make_async_copy(slots_v, slots, tb.at[0])
    l_slots.start()
    rank = jnp.where(lane == going[1], 1, jnp.where(lane == going[2], 2, 0))
    slot_of = CAP * jnp.where(lane1 < TILES, mine, 0) + jnp.max(rank, axis=0, keepdims=True)
    chains_v[SLOT_OF : SLOT_OF + 1] = slot_of

    def slot_target(n, k):
        tile = slots[SHARDS + n, k]
        return tile, targets[TILES * n + jnp.maximum(tile, 0)]

    def chain(outer, inner, label, none, prev_row, last_row):
        def gather(i, labels):
            for j in range(inner):
                labels = jnp.where(lane1 == inner * i + j, label(i, j), labels)
            return labels

        labels = lax.fori_loop(0, outer, gather, jnp.full((1, BLOCK), -2, jnp.int32))

        def link(i, carry):
            prev, last = carry
            for j in range(inner):
                at, here = inner * i + j, label(i, j)
                prev = jnp.where((labels == here) & (lane1 > at), at, prev)
                last = jnp.where(lane1 == here, at, last)
            return prev, last

        empty = jnp.full((1, BLOCK), none, jnp.int32)
        prev, last = lax.fori_loop(0, outer, link, (empty, empty))
        chains_v[prev_row : prev_row + 1] = prev
        chains_v[last_row : last_row + 1] = last

    def source(i, j):
        return sources[TILES * s + 4 * i + j]

    def target(i, j):
        tile, at = slot_target(i, j)
        return jnp.where(tile < 0, -1, at)

    def key(i, j):
        return keys[j, (h + 1 + i) % QB]

    l_slots.wait()
    recv_all(c_f, HEADS)
    ring_right(0).start()
    ring_left(0).start()
    to_sib(0).start()
    l_tw.wait()

    @each(0, TILES, 8)
    def _(t):
        part[t] = nt(f_t[sources[TILES * s + t]], twv[t]).astype(BF16)

    @each(0, SHARDS, 4)
    def _(n):
        for k in range(CAP):
            outg[CAP * n + k] = part[slots[n, k]]

    start_all(c_p, SHARDS)
    arr[pl.ds(s * CAP, CAP)] = outg[pl.ds(s * CAP, CAP)]
    chain(TILES // 4, 4, source, TILES, PREV_SRC, LAST_SRC)
    ring_step(1)
    chain(QB, KMAX, key, QB * KMAX, PREV_KEY, LAST_KEY)
    ring_step(2)
    each(1, 5)(lambda d: c_q(d).start())
    chain(SHARDS, CAP, target, SLOTS, PREV_TGT, LAST_TGT)
    l_chains = pltpu.make_async_copy(chains_v, chains, tb.at[1])
    l_chains.start()
    ring_step(3)
    each(5, 9)(lambda d: c_q(d).start())
    ring_step(4)
    each(9, HEADS)(lambda d: c_q(d).start())
    each(0, 8)(lambda k: to_sib(k).wait_recv())
    l_chains.wait()

    @each(0, SHARDS, 4)
    def _(n):
        for k in range(CAP):
            rep[CAP * n + k] = u_t[slot_target(n, k)[1], my_rows]

    start_all(c_e, SHARDS)
    retd[pl.ds(s * CAP, CAP)] = rep[pl.ds(s * CAP, CAP)]

    l_ow.wait()

    @each(0, QB, 2)
    def _(b):
        g_t[b] = nn(owv[my_rows], u_t[b]).astype(BF16)

    recv_all(c_p, SHARDS)

    @each(0, SLOTS, 8)
    def _(p):
        run_t[p] = arr[p].astype(F32) + run_t[chains[PREV_TGT, p]]

    @each(1, HEADS)
    def _(d):
        b = (h + d) % HEADS
        s_m[b] = run_t[chains[LAST_TGT, b]].astype(BF16)
        c_m(d).start()

    r_m[h] = run_t[chains[LAST_TGT, h]].astype(BF16)

    recv_all(c_q, HEADS)

    @each(0, QB, 2)
    def _(b):
        kv[b] = q_t[b, HS:].T

    scale = HS ** (-0.5)
    pad = jnp.zeros((HS, BLOCK), BF16)

    def attend(i):
        r = (h + 1 + i) % QB
        q = q_t[r, :HS]
        g = g_t[r]
        blocks = [keys[j, r] for j in range(KMAX)]
        count = counts[r]
        qg = jnp.concatenate(
            [jnp.concatenate([q, pad], axis=1), jnp.concatenate([pad, g], axis=1)], axis=0
        )
        both = [nn(kv[blocks[j]], qg) for j in range(KMAX)]
        scores = [
            both[j][:, :BLOCK] * scale + jnp.where(j < count, 0.0, -jnp.inf).astype(F32)
            for j in range(KMAX)
        ]
        grad_prob = [both[j][:, BLOCK:] for j in range(KMAX)]
        top = functools.reduce(
            jnp.maximum, [jnp.max(sc, axis=0, keepdims=True) for sc in scores]
        )
        expo = [jnp.exp(sc - top) for sc in scores]
        total = sum(jnp.sum(e, axis=0, keepdims=True) for e in expo)
        inverse = 1.0 / total
        prob = [e * inverse for e in expo]
        delta = sum(
            jnp.sum(a * b, axis=0, keepdims=True) for a, b in zip(prob, grad_prob)
        )
        prob_b = jnp.concatenate([a.astype(BF16) for a in prob], axis=0)
        dscore = jnp.concatenate(
            [(a * (b - delta) * scale).astype(BF16) for a, b in zip(prob, grad_prob)], axis=0
        )
        keys_t = jnp.concatenate([q_t[b, HS : 2 * HS] for b in blocks], axis=1)
        values_t = jnp.concatenate([q_t[b, 2 * HS :] for b in blocks], axis=1)
        s_a[r, :HS] = nn(values_t, prob_b).astype(BF16)
        s_a[r, HS:] = nn(keys_t, dscore).astype(BF16)
        term_k = nt(q, dscore)
        term_v = nt(g, prob_b)
        for j in range(KMAX):
            before = chains[PREV_KEY, KMAX * i + j]
            lanes = slice(BLOCK * j, BLOCK * (j + 1))
            run_k[KMAX * i + j] = term_k[:, lanes] + run_k[before]
            run_v[KMAX * i + j] = term_v[:, lanes] + run_v[before]

    @each(0, QB - 1)
    def _(i):
        attend(i)
        c_a(i + 1).start()

    attend(QB - 1)
    r_a[h] = s_a[h]

    @each(1, HEADS)
    def _(d):
        b = (h + d) % HEADS
        last = chains[LAST_KEY, b]
        s_kv[b, :HS] = run_k[last].astype(BF16)
        s_kv[b, HS:] = run_v[last].astype(BF16)
        c_kv(d).start()

    last_own = chains[LAST_KEY, h]
    s_kv[h, :HS] = run_k[last_own].astype(BF16)
    s_kv[h, HS:] = run_v[last_own].astype(BF16)
    o_kv = pltpu.make_async_copy(s_kv.at[h], r_kv.at[h], out.at[0])
    o_kv.start()

    wg_acc[...] = nt(u_t[0], s_a[0, :HS])

    @each(1, QB)
    def _(b):
        wg_acc[...] += nt(u_t[b], s_a[b, :HS])

    columns = D // SHARDS
    for n in range(SHARDS):
        wg_p[(n % NX) * NZ + n // NX] = wg_acc[columns * n : columns * (n + 1)]

    def c_x(d):
        to = (x + d) % NX
        return remote(
            wg_p.at[pl.ds(to * NZ, NZ)], wx_r.at[x], xs.at[d], xr.at[d], "seq", z * NX + to
        )

    def c_z(d):
        to = (z + d) % NZ
        return remote(wz_p.at[to], wz_r.at[z], zs.at[d], zr.at[d], "seq", to * NX + x)

    start_all(c_x, NX)
    wx_r[x] = wg_p[pl.ds(x * NZ, NZ)]

    recv_all(c_x, NX)
    wz_p[...] = wx_r[0] + wx_r[1] + wx_r[2] + wx_r[3]
    wz_r[z] = wz_p[z]

    recv_all(c_e, SHARDS)
    start_all(c_z, NZ)

    @each(0, TILES, 8)
    def _(t):
        run_s[t] = nn(retd[chains[SLOT_OF, t]], twv[t])

    @each(0, TILES, 8)
    def _(t):
        run_s[t] = run_s[t] + run_s[chains[PREV_SRC, t]]

    @each(1, HEADS)
    def _(d):
        b = (h + d) % HEADS
        s_f[b] = run_s[chains[LAST_SRC, b]].astype(BF16)
        c_df(d).start()

    s_f[h] = run_s[chains[LAST_SRC, h]].astype(BF16)
    o_f = pltpu.make_async_copy(s_f.at[h], r_f.at[h], out.at[1])
    o_f.start()

    recv_all(c_a, HEADS)
    o_q = pltpu.make_async_copy(r_a.at[:, pl.ds(HS, HS)], q_out, out.at[3])
    o_q.start()
    recv_all(c_m, HEADS)
    per = HEADS // 2
    acc = jnp.zeros((BLOCK, D), F32)
    for i in range(2):
        wide = jnp.concatenate([r_a[per * i + k, :HS] for k in range(per)], axis=0).T
        acc = acc + nn(wide, owv[half * i : half * (i + 1)])
    mixed = [
        jnp.concatenate([r_m[per * i + k] for k in range(per)], axis=0).T for i in range(2)
    ]
    lo_v[...] = (acc + jnp.concatenate(mixed, axis=1).astype(F32)).astype(BF16)
    o_lo = pltpu.make_async_copy(lo_v, lo_out, out.at[4])
    o_lo.start()
    recv_all(c_z, NZ)
    total = wz_r[0]
    for n in range(1, NZ):
        total = total + wz_r[n]
    wg_v[...] = total * (1.0 / math.sqrt(SHARDS * QB * BLOCK))
    o_wg = pltpu.make_async_copy(wg_v, wg_out, out.at[2])
    o_wg.start()

    recv_all(c_kv, HEADS)
    recv_all(c_df, HEADS)
    for copy in (o_kv, o_f, o_wg, o_q, o_lo):
        copy.wait()

    for copy in (c_f, c_q, c_a, c_kv, c_df, c_m):
        send_all(copy, HEADS)
    send_all(c_p, SHARDS)
    send_all(c_e, SHARDS)
    send_all(c_x, NX)
    send_all(c_z, NZ)
    for i in range(4):
        ring_right(i).wait_send()
        ring_left(i).wait_send()
    each(0, 8)(lambda k: to_sib(k).wait_send())


def finish(
    lo, q, kv, f, wg, lo_out, gp_out, wg_out, lo_v, q_v, kv_v, f_v, wg_v, gp_v, sem
):
    loads = [
        pltpu.make_async_copy(a, b, sem.at[n])
        for n, (a, b) in enumerate(((lo, lo_v), (wg, wg_v), (q, q_v), (kv, kv_v), (f, f_v)))
    ]
    for copy in loads:
        copy.start()
    stores = [
        pltpu.make_async_copy(a, b, sem.at[9 + n])
        for n, (a, b) in enumerate(((lo_v, lo_out), (wg_v, wg_out)))
    ]
    for copy in loads:
        copy.wait()
    for copy in stores:
        copy.start()
    wide = 8 * HS
    for i in range(HEADS // 2):
        rows = []
        for n in (2 * i, 2 * i + 1):
            rows += [q_v[n], kv_v[n], f_v[n]]
        lanes = pl.ds(wide * i, wide)
        gp_v[:, lanes] = jnp.concatenate(rows, axis=0).T
        if i % 2:
            lanes = pl.ds(wide * (i - 1), 2 * wide)
            stores.append(
                pltpu.make_async_copy(gp_v.at[:, lanes], gp_out.at[:, lanes], sem.at[5 + i // 2])
            )
            stores[-1].start()
    for copy in stores:
        copy.wait()


def body(
    projected, upstream, out_weight, tile_weights, tile_owner,
    source_block, target_block, key_blocks, key_count,
):
    any_space = pl.BlockSpec(memory_space=pl.ANY)

    def buf(*shape, dtype=BF16):
        return pltpu.VMEM(shape, dtype)

    def sems(n):
        return pltpu.SemaphoreType.DMA((n,))

    tiles = (HS, BLOCK)
    tall = jax.ShapeDtypeStruct((HEADS, *tiles), BF16)
    columns = D // SHARDS
    lo, q, kv, f, wg = pl.pallas_call(
        kernel,
        out_shape=(
            jax.ShapeDtypeStruct((BLOCK, D), BF16),
            tall,
            jax.ShapeDtypeStruct((HEADS, 2 * HS, BLOCK), BF16),
            tall,
            jax.ShapeDtypeStruct((columns, HS), F32),
        ),
        in_specs=[any_space] * 9,
        out_specs=(any_space,) * 5,
        scratch_shapes=[
            buf(1, SHARDS * TILES, dtype=jnp.int32), pltpu.SMEM((SHARDS * TILES,), jnp.int32),
            pltpu.SMEM((SHARDS * TILES,), jnp.int32), pltpu.SMEM((KMAX, QB), jnp.int32),
            pltpu.SMEM((QB,), jnp.int32), buf(BLOCK, D), buf(columns, HS, dtype=F32),
            buf(SHARDS, BLOCK, dtype=jnp.int32), buf(2 * SHARDS, BLOCK, dtype=jnp.int32),
            pltpu.SMEM((2 * SHARDS, BLOCK), jnp.int32),
            buf(8, BLOCK, dtype=jnp.int32), pltpu.SMEM((8, BLOCK), jnp.int32),
            buf(BLOCK, 4 * D), buf(BLOCK, D), buf(D, D), buf(TILES, BLOCK, BLOCK),
            buf(HEADS, *tiles), buf(HEADS, 3 * HS, BLOCK),
            buf(HEADS, *tiles), buf(HEADS, 3 * HS, BLOCK),
            buf(QB, D, BLOCK), buf(QB, *tiles), buf(QB, BLOCK, 2 * HS),
            buf(TILES, *tiles), buf(SLOTS, *tiles), buf(SLOTS, *tiles),
            buf(SLOTS, *tiles), buf(SLOTS, *tiles),
            buf(SLOTS + 1, *tiles, dtype=F32), buf(TILES + 1, *tiles, dtype=F32),
            buf(QB * KMAX + 1, *tiles, dtype=F32), buf(QB * KMAX + 1, *tiles, dtype=F32),
            buf(HEADS, 2 * HS, BLOCK), buf(HEADS, 2 * HS, BLOCK),
            buf(HEADS, *tiles), buf(HEADS, *tiles),
            buf(HEADS, 2 * HS, BLOCK), buf(HEADS, *tiles),
            buf(D, HS, dtype=F32), buf(SHARDS, D // SHARDS, HS, dtype=F32),
            buf(NX, NZ, D // SHARDS, HS, dtype=F32),
            buf(NZ, D // SHARDS, HS, dtype=F32), buf(NZ, D // SHARDS, HS, dtype=F32),
            sems(9), sems(2), sems(5), sems(HEADS), sems(HEADS), sems(HEADS), sems(HEADS),
            sems(4), sems(4), sems(4), sems(4), sems(8), sems(8),
            sems(SHARDS), sems(SHARDS), sems(SHARDS), sems(SHARDS),
            sems(HEADS), sems(HEADS), sems(HEADS), sems(HEADS),
            sems(HEADS), sems(HEADS), sems(HEADS), sems(HEADS),
            sems(NX), sems(NX), sems(NZ), sems(NZ),
        ],
        compiler_params=pltpu.CompilerParams(
            collective_id=0, has_side_effects=True, vmem_limit_bytes=61 << 20
        ),
    )(
        tile_owner.T, source_block, target_block, key_blocks.T, key_count,
        projected, upstream, out_weight, tile_weights,
    )
    layer_out, grad_projected, weight_grad = pl.pallas_call(
        finish,
        out_shape=(
            jax.ShapeDtypeStruct((BLOCK, D), BF16),
            jax.ShapeDtypeStruct((BLOCK, 4 * D), BF16),
            jax.ShapeDtypeStruct((columns, HS), F32),
        ),
        in_specs=[any_space] * 5,
        out_specs=(any_space,) * 3,
        scratch_shapes=[
            buf(BLOCK, D), buf(HEADS, *tiles), buf(HEADS, 2 * HS, BLOCK), buf(HEADS, *tiles),
            buf(columns, HS, dtype=F32), buf(BLOCK, 4 * D), sems(11),
        ],
        compiler_params=pltpu.CompilerParams(vmem_limit_bytes=61 << 20),
    )(lo, q, kv, f, wg)
    return layer_out, grad_projected, weight_grad.T


def solution(mesh):
    in_specs = (
        P(("seq", "head"), None), P(("seq", "head"), None), P(), P("seq", None, None),
        P(), P(), P(), P("seq", None), P("seq"),
    )
    out_specs = (P(("seq", "head"), None), P(("seq", "head"), None), P("head", "seq"))
    return jax.shard_map(body, mesh=mesh, in_specs=in_specs, out_specs=out_specs, check_vma=False)
```

```python
import functools
import math

import jax
import jax.numpy as jnp
from jax import lax
from jax.experimental import pallas as pl
from jax.experimental.pallas import tpu as pltpu
from jax.sharding import PartitionSpec as P

MESH = pl.DeviceIdType.MESH
HEADS = 16
BLOCK = 128
CAP = 3
HS = 48
D = 768
QB = 16
KMAX = 4
TILES = 48
SHARDS = 32
SLOTS = SHARDS * CAP
NX = 4
NZ = 8
F32 = jnp.float32
BF16 = jnp.bfloat16

PREV_SRC, LAST_SRC, PREV_TGT, LAST_TGT, PREV_KEY, LAST_KEY = range(6)
FEW, MANY = 16, 32


def nn(a, b):
    return lax.dot_general(a, b, (((1,), (0,)), ((), ())), preferred_element_type=F32)


def nt(a, b):
    return lax.dot_general(a, b, (((1,), (1,)), ((), ())), preferred_element_type=F32)


def each(start, stop, unroll=1):
    def run(f):
        def step(i, carry):
            f(i)
            return carry

        lax.fori_loop(start, stop, step, 0, unroll=unroll)

    return run


def kernel(
    own_in, sources_in, targets_in, keys_in, counts_in, pj, up, ow, tw,
    lo_out, q_out, r_kv, r_fa, r_fb, wg_out,
    own, sources, targets, keys, counts, lo_v, wg_v,
    own_m, slots_v, slots, chains_v, chains,
    pjv, upv, owv, twv,
    p_fa, p_fb, p_q, f_ta, f_tb, q_t, u_t, g_t, kv,
    part_a, part_b, outg_a, outg_b, arr_a, arr_b, rep_a, rep_b, ret_a, ret_b,
    run_t, run_sa, run_sb, run_k, run_v,
    s_a, s_kv, s_fa, s_fb, s_m, r_a, r_m,
    wg_acc, wg_p, wx_r, wz_p, wz_r,
    ld, tb, out, fas, far, fbs, fbr, qs, qr, rs, rr, ls, lr, bs, br,
    pas, par, pbs, pbr, eas, ear, ebs, ebr,
    as_, ar, ks, kr, has, har, hbs, hbr, ms, mr, xs, xr, zs, zr,
):
    s = lax.axis_index("seq")
    h = lax.axis_index("head")
    z = s // NX
    x = s % NX
    sib = h + 1 - 2 * (h % 2)
    right, left = (h + 2) % HEADS, (h + HEADS - 2) % HEADS
    my_rows = pl.ds(pl.multiple_of(h * HS, 16), HS)
    my_many = pl.ds(pl.multiple_of(h * HS, 16), MANY)
    my_few = pl.ds(pl.multiple_of(h * HS + MANY, 16), FEW)

    def remote(src, dst, send, recv, axis, peer):
        return pltpu.make_async_remote_copy(
            src_ref=src, dst_ref=dst, send_sem=send, recv_sem=recv,
            device_id={axis: peer}, device_id_type=MESH,
        )

    def head_copy(src, dst, send, recv):
        def at(d):
            peer = (h + d) % HEADS
            return remote(src.at[peer], dst.at[h], send.at[d], recv.at[d], "head", peer)

        return at

    def seq_copy(src, dst, send, recv):
        def at(d):
            peer = (s + d) % SHARDS
            return remote(
                src.at[pl.ds(peer * CAP, CAP)], dst.at[pl.ds(s * CAP, CAP)],
                send.at[d], recv.at[d], "seq", peer,
            )

        return at

    c_fa = head_copy(p_fa, f_ta, fas, far)
    c_fb = head_copy(p_fb, f_tb, fbs, fbr)
    c_q = head_copy(p_q, q_t, qs, qr)
    c_a = head_copy(s_a, r_a, as_, ar)
    c_kv = head_copy(s_kv, r_kv, ks, kr)
    c_dfa = head_copy(s_fa, r_fa, has, har)
    c_dfb = head_copy(s_fb, r_fb, hbs, hbr)
    c_m = head_copy(s_m, r_m, ms, mr)
    c_pa = seq_copy(outg_a, arr_a, pas, par)
    c_pb = seq_copy(outg_b, arr_b, pbs, pbr)
    c_ea = seq_copy(rep_a, ret_a, eas, ear)
    c_eb = seq_copy(rep_b, ret_b, ebs, ebr)

    def start_all(copy, n):
        each(1, n)(lambda d: copy(d).start())

    def recv_all(copy, n):
        each(1, n)(lambda d: copy(d).wait_recv())

    def send_all(copy, n):
        each(1, n)(lambda d: copy(d).wait_send())

    half = D // 2
    first, second = pl.ds(0, half), pl.ds(half, half)

    def ring_right(i, lead):
        ref = u_t.at[(h + HEADS - 2 * i) % HEADS, first if lead else second]
        n = 2 * i + 1 - lead
        return remote(ref, ref, rs.at[n], rr.at[n], "head", right)

    def ring_left(i, lead):
        ref = u_t.at[(h + 2 * i) % HEADS, second if lead else first]
        n = 2 * i + 1 - lead
        return remote(ref, ref, ls.at[n], lr.at[n], "head", left)

    def to_sib(k):
        ref = u_t.at[(h + 2 * k) % HEADS]
        return remote(ref, ref, bs.at[k], br.at[k], "head", sib)

    l_up = pltpu.make_async_copy(up, upv, ld.at[0])
    l_pj = pltpu.make_async_copy(pj, pjv, ld.at[1])
    l_tw = pltpu.make_async_copy(tw, twv, ld.at[2])
    l_ow = pltpu.make_async_copy(ow, owv, ld.at[3])
    small = (
        (own_in, own), (sources_in, sources), (targets_in, targets), (keys_in, keys),
        (counts_in, counts),
    )
    l_small = [pltpu.make_async_copy(a, b, ld.at[4 + n]) for n, (a, b) in enumerate(small)]
    l_pj.start()
    l_up.start()
    barrier = pltpu.get_barrier_semaphore()
    for d in range(1, HEADS):
        pl.semaphore_signal(
            barrier, inc=1, device_id={"head": (h + d) % HEADS}, device_id_type=MESH
        )
    for d in range(1, SHARDS):
        pl.semaphore_signal(
            barrier, inc=1, device_id={"seq": (s + d) % SHARDS}, device_id_type=MESH
        )
    for load in (*l_small, l_tw, l_ow):
        load.start()
    l_pj.wait()
    for i in range(HEADS // 2):
        pair = pjv[:, 8 * HS * i : 8 * HS * (i + 1)].T
        for k in range(2):
            p_q[2 * i + k] = pair[4 * HS * k : 4 * HS * k + 3 * HS]
            p_fa[2 * i + k] = pair[4 * HS * k + 3 * HS : 4 * HS * k + 3 * HS + FEW]
            p_fb[2 * i + k] = pair[4 * HS * k + 3 * HS + FEW : 4 * HS * (k + 1)]
    pl.semaphore_wait(barrier, HEADS + SHARDS - 2)

    start_all(c_fa, HEADS)
    start_all(c_fb, HEADS)
    f_ta[h] = p_fa[h]
    f_tb[h] = p_fb[h]
    q_t[h] = p_q[h]
    l_up.wait()
    for i in range(2):
        u_t[h, half * i : half * (i + 1)] = upv[:, half * i : half * (i + 1)].T
    run_t[SLOTS] = jnp.zeros((HS, BLOCK), F32)
    run_sa[SLOTS] = jnp.zeros((MANY, BLOCK), F32)
    run_sb[SLOTS] = jnp.zeros((FEW, BLOCK), F32)
    run_k[QB * KMAX] = jnp.zeros((HS, BLOCK), F32)
    run_v[QB * KMAX] = jnp.zeros((HS, BLOCK), F32)

    def ring_step(i):
        for lead in (1, 0) if i < 4 else (1,):
            for ring in (ring_right, ring_left):
                ring(i - 1, lead).wait_recv()
                if i < 3 or (lead and i < 4):
                    ring(i, lead).start()
        if i < 4:
            to_sib(8 - i).start()
        to_sib(i).start()

    for load in l_small:
        load.wait()
    for n in range(SHARDS):
        own_m[n : n + 1, :TILES] = own[:, TILES * n : TILES * (n + 1)]
    lane = lax.broadcasted_iota(jnp.int32, (SHARDS, BLOCK), 1)
    row = lax.broadcasted_iota(jnp.int32, (SHARDS, BLOCK), 0)
    lane1 = lax.broadcasted_iota(jnp.int32, (1, BLOCK), 1)

    def first_three(same):
        found = []
        for k in range(CAP):
            later = same & (lane > found[-1]) if k else same
            found.append(jnp.min(jnp.where(later, lane, 999), axis=1, keepdims=True))
        return found

    def in_lanes(found, none):
        listed = jnp.where(lane == 0, found[0], jnp.where(lane == 1, found[1], found[2]))
        return jnp.where(listed == 999, none, listed)

    mine = own_m[pl.ds(s, 1), :]
    going = first_three((mine == row) & (lane < TILES))
    coming = first_three((own_m[...] == s) & (lane < TILES))
    slots_v[:SHARDS] = in_lanes(going, -1)
    slots_v[SHARDS:] = in_lanes(coming, -1)
    l_slots = pltpu.make_async_copy(slots_v, slots, tb.at[0])
    l_slots.start()
    def slot_target(n, k):
        tile = slots[SHARDS + n, k]
        return tile, targets[TILES * n + jnp.maximum(tile, 0)]

    def chain(outer, inner, label, none, prev_row, last_row):
        def gather(i, labels):
            for j in range(inner):
                labels = jnp.where(lane1 == inner * i + j, label(i, j), labels)
            return labels

        labels = lax.fori_loop(0, outer, gather, jnp.full((1, BLOCK), -2, jnp.int32))

        def link(i, carry):
            prev, last = carry
            for j in range(inner):
                at, here = inner * i + j, label(i, j)
                prev = jnp.where((labels == here) & (lane1 > at), at, prev)
                last = jnp.where(lane1 == here, at, last)
            return prev, last

        empty = jnp.full((1, BLOCK), none, jnp.int32)
        prev, last = lax.fori_loop(0, outer, link, (empty, empty))
        chains_v[prev_row : prev_row + 1] = prev
        chains_v[last_row : last_row + 1] = last

    def source(d, k):
        tile = slots[(s + SHARDS - d) % SHARDS, k]
        return jnp.where(tile < 0, -1, sources[TILES * s + jnp.maximum(tile, 0)])

    def target(i, j):
        tile, at = slot_target(i, j)
        return jnp.where(tile < 0, -1, at)

    def key(i, j):
        return keys[j, (h + 1 + i) % QB]

    l_slots.wait()
    l_tw.wait()

    def products(f_t, part, outg):
        @each(0, TILES, 8)
        def _(t):
            part[t] = nt(f_t[sources[TILES * s + t]], twv[t]).astype(BF16)

        @each(0, SHARDS, 4)
        def _(n):
            for k in range(CAP):
                outg[CAP * n + k] = part[jnp.maximum(slots[n, k], 0)]

    own_slots = pl.ds(s * CAP, CAP)
    recv_all(c_fa, HEADS)
    products(f_ta, part_a, outg_a)
    start_all(c_pa, SHARDS)
    recv_all(c_fb, HEADS)
    for lead in (1, 0):
        ring_right(0, lead).start()
        ring_left(0, lead).start()
    to_sib(0).start()
    products(f_tb, part_b, outg_b)
    start_all(c_pb, SHARDS)
    each(1, 4)(lambda d: c_q(d).start())
    arr_a[own_slots] = outg_a[own_slots]
    arr_b[own_slots] = outg_b[own_slots]
    chain(SHARDS, CAP, source, SLOTS, PREV_SRC, LAST_SRC)
    ring_step(1)
    chain(QB, KMAX, key, QB * KMAX, PREV_KEY, LAST_KEY)
    ring_step(2)
    each(4, 8)(lambda d: c_q(d).start())
    chain(SHARDS, CAP, target, SLOTS, PREV_TGT, LAST_TGT)
    l_chains = pltpu.make_async_copy(chains_v, chains, tb.at[1])
    l_chains.start()
    ring_step(3)
    each(8, HEADS)(lambda d: c_q(d).start())
    ring_step(4)
    each(0, 8)(lambda k: to_sib(k).wait_recv())
    l_chains.wait()

    def replies(rep, ret, rows):
        @each(0, SHARDS, 4)
        def _(n):
            for k in range(CAP):
                rep[CAP * n + k] = u_t[slot_target(n, k)[1], rows]

        ret[own_slots] = rep[own_slots]

    replies(rep_a, ret_a, my_many)
    start_all(c_ea, SHARDS)
    replies(rep_b, ret_b, my_few)
    start_all(c_eb, SHARDS)

    l_ow.wait()

    @each(0, QB, 2)
    def _(b):
        g_t[b] = nn(owv[my_rows], u_t[b]).astype(BF16)

    recv_all(c_pa, SHARDS)
    recv_all(c_pb, SHARDS)

    @each(0, SLOTS, 8)
    def _(p):
        before = run_t[chains[PREV_TGT, p]]
        run_t[p, :FEW] = arr_a[p].astype(F32) + before[:FEW]
        run_t[p, FEW:] = arr_b[p].astype(F32) + before[FEW:]

    @each(1, HEADS)
    def _(d):
        b = (h + d) % HEADS
        s_m[b] = run_t[chains[LAST_TGT, b]].astype(BF16)
        c_m(d).start()

    r_m[h] = run_t[chains[LAST_TGT, h]].astype(BF16)

    for copy in (c_fa, c_fb):
        send_all(copy, HEADS)
    for copy in (c_pa, c_pb):
        send_all(copy, SHARDS)
    for i in range(4):
        for lead in (1, 0) if i < 3 else (1,):
            ring_right(i, lead).wait_send()
            ring_left(i, lead).wait_send()
    each(0, 8)(lambda k: to_sib(k).wait_send())
    recv_all(c_q, HEADS)

    @each(0, QB, 2)
    def _(b):
        kv[b] = q_t[b, HS:].T

    scale = HS ** (-0.5)
    pad = jnp.zeros((HS, BLOCK), BF16)

    def attend(i):
        r = (h + 1 + i) % QB
        q = q_t[r, :HS]
        g = g_t[r]
        blocks = [keys[j, r] for j in range(KMAX)]
        count = counts[r]
        qg = jnp.concatenate(
            [jnp.concatenate([q, pad], axis=1), jnp.concatenate([pad, g], axis=1)], axis=0
        )
        both = [nn(kv[blocks[j]], qg) for j in range(KMAX)]
        scores = [
            both[j][:, :BLOCK] * scale + jnp.where(j < count, 0.0, -jnp.inf).astype(F32)
            for j in range(KMAX)
        ]
        grad_prob = [both[j][:, BLOCK:] for j in range(KMAX)]
        top = functools.reduce(
            jnp.maximum, [jnp.max(sc, axis=0, keepdims=True) for sc in scores]
        )
        expo = [jnp.exp(sc - top) for sc in scores]
        total = sum(jnp.sum(e, axis=0, keepdims=True) for e in expo)
        inverse = 1.0 / total
        prob = [e * inverse for e in expo]
        delta = sum(
            jnp.sum(a * b, axis=0, keepdims=True) for a, b in zip(prob, grad_prob)
        )
        prob_b = jnp.concatenate([a.astype(BF16) for a in prob], axis=0)
        dscore = jnp.concatenate(
            [(a * (b - delta) * scale).astype(BF16) for a, b in zip(prob, grad_prob)], axis=0
        )
        keys_t = jnp.concatenate([q_t[b, HS : 2 * HS] for b in blocks], axis=1)
        values_t = jnp.concatenate([q_t[b, 2 * HS :] for b in blocks], axis=1)
        s_a[r, :HS] = nn(values_t, prob_b).astype(BF16)
        s_a[r, HS:] = nn(keys_t, dscore).astype(BF16)
        term_k = nt(q, dscore)
        term_v = nt(g, prob_b)
        for j in range(KMAX):
            before = chains[PREV_KEY, KMAX * i + j]
            lanes = slice(BLOCK * j, BLOCK * (j + 1))
            run_k[KMAX * i + j] = term_k[:, lanes] + run_k[before]
            run_v[KMAX * i + j] = term_v[:, lanes] + run_v[before]

    @each(0, QB // 4)
    def _(g):
        for j in range(4):
            attend(4 * g + j)
        for j in range(3):
            c_a(4 * g + j + 1).start()

        @pl.when(g < QB // 4 - 1)
        def _():
            c_a(4 * g + 4).start()

    r_a[h] = s_a[h]

    @each(1, HEADS)
    def _(d):
        b = (h + d) % HEADS
        last = chains[LAST_KEY, b]
        s_kv[b, :HS] = run_k[last].astype(BF16)
        s_kv[b, HS:] = run_v[last].astype(BF16)
        c_kv(d).start()

    last_own = chains[LAST_KEY, h]
    s_kv[h, :HS] = run_k[last_own].astype(BF16)
    s_kv[h, HS:] = run_v[last_own].astype(BF16)
    o_kv = pltpu.make_async_copy(s_kv.at[h], r_kv.at[h], out.at[0])
    o_kv.start()

    wg_acc[...] = nt(u_t[0], s_a[0, :HS])

    @each(1, QB)
    def _(b):
        wg_acc[...] += nt(u_t[b], s_a[b, :HS])

    columns = D // SHARDS
    for n in range(SHARDS):
        wg_p[(n % NX) * NZ + n // NX] = wg_acc[columns * n : columns * (n + 1)]

    def c_x(d):
        to = (x + d) % NX
        return remote(
            wg_p.at[pl.ds(to * NZ, NZ)], wx_r.at[x], xs.at[d], xr.at[d], "seq", z * NX + to
        )

    def c_z(d):
        to = (z + d) % NZ
        return remote(wz_p.at[to], wz_r.at[z], zs.at[d], zr.at[d], "seq", to * NX + x)

    start_all(c_x, NX)
    wx_r[x] = wg_p[pl.ds(x * NZ, NZ)]

    group = 4

    def back(copy, ret, run, sent):
        def some(g, first):
            for j in range(first, group):
                copy(group * g + j).wait_recv()
            for j in range(group):
                d = group * g + j
                n = (s + SHARDS - d) % SHARDS
                for k in range(CAP):
                    q = CAP * d + k
                    term = nn(ret[CAP * n + k], twv[jnp.maximum(slots[n, k], 0)])
                    run[q] = term + run[chains[PREV_SRC, q]]

        some(0, 1)
        each(1, SHARDS // group)(lambda g: some(g, 0))

        @each(0, QB, 4)
        def _(b):
            sent[b] = run[chains[LAST_SRC, b]].astype(BF16)

    back(c_ea, ret_a, run_sa, s_fa)
    start_all(c_dfa, HEADS)
    o_fa = pltpu.make_async_copy(s_fa.at[h], r_fa.at[h], out.at[1])
    o_fa.start()
    recv_all(c_x, NX)
    wz_p[...] = wx_r[0] + wx_r[1] + wx_r[2] + wx_r[3]
    wz_r[z] = wz_p[z]
    back(c_eb, ret_b, run_sb, s_fb)
    start_all(c_dfb, HEADS)
    o_fb = pltpu.make_async_copy(s_fb.at[h], r_fb.at[h], out.at[5])
    o_fb.start()
    start_all(c_z, NZ)

    recv_all(c_a, HEADS)
    o_q = pltpu.make_async_copy(r_a.at[:, pl.ds(HS, HS)], q_out, out.at[3])
    o_q.start()
    recv_all(c_m, HEADS)
    per = HEADS // 2
    acc = jnp.zeros((BLOCK, D), F32)
    for i in range(2):
        wide = jnp.concatenate([r_a[per * i + k, :HS] for k in range(per)], axis=0).T
        acc = acc + nn(wide, owv[half * i : half * (i + 1)])
    mixed = [
        jnp.concatenate([r_m[per * i + k] for k in range(per)], axis=0).T for i in range(2)
    ]
    lo_v[...] = (acc + jnp.concatenate(mixed, axis=1).astype(F32)).astype(BF16)
    o_lo = pltpu.make_async_copy(lo_v, lo_out, out.at[4])
    o_lo.start()
    recv_all(c_z, NZ)
    total = wz_r[0]
    for n in range(1, NZ):
        total = total + wz_r[n]
    wg_v[...] = total * (1.0 / math.sqrt(SHARDS * QB * BLOCK))
    o_wg = pltpu.make_async_copy(wg_v, wg_out, out.at[2])
    o_wg.start()

    for copy in (c_q, c_m, c_a, c_kv):
        send_all(copy, HEADS)
    for copy in (c_ea, c_eb):
        send_all(copy, SHARDS)
    send_all(c_x, NX)
    recv_all(c_kv, HEADS)
    recv_all(c_dfa, HEADS)
    recv_all(c_dfb, HEADS)
    for copy in (o_kv, o_fa, o_fb, o_wg, o_q, o_lo):
        copy.wait()

    for copy in (c_dfa, c_dfb):
        send_all(copy, HEADS)
    send_all(c_z, NZ)


def finish(
    lo, q, kv, fa, fb, wg, lo_out, gp_out, wg_out,
    lo_v, q_v, kv_v, fa_v, fb_v, wg_v, gp_v, sem,
):
    loads = [
        pltpu.make_async_copy(a, b, sem.at[n])
        for n, (a, b) in enumerate(
            ((lo, lo_v), (wg, wg_v), (q, q_v), (kv, kv_v), (fa, fa_v), (fb, fb_v))
        )
    ]
    for copy in loads:
        copy.start()
    stores = [
        pltpu.make_async_copy(a, b, sem.at[10 + n])
        for n, (a, b) in enumerate(((lo_v, lo_out), (wg_v, wg_out)))
    ]
    for copy in loads:
        copy.wait()
    for copy in stores:
        copy.start()
    wide = 8 * HS
    for i in range(HEADS // 2):
        rows = []
        for n in (2 * i, 2 * i + 1):
            rows += [q_v[n], kv_v[n], fa_v[n], fb_v[n]]
        lanes = pl.ds(wide * i, wide)
        gp_v[:, lanes] = jnp.concatenate(rows, axis=0).T
        if i % 2:
            lanes = pl.ds(wide * (i - 1), 2 * wide)
            stores.append(
                pltpu.make_async_copy(gp_v.at[:, lanes], gp_out.at[:, lanes], sem.at[6 + i // 2])
            )
            stores[-1].start()
    for copy in stores:
        copy.wait()


def body(
    projected, upstream, out_weight, tile_weights, tile_owner,
    source_block, target_block, key_blocks, key_count,
):
    any_space = pl.BlockSpec(memory_space=pl.ANY)

    def buf(*shape, dtype=BF16):
        return pltpu.VMEM(shape, dtype)

    def sems(n):
        return pltpu.SemaphoreType.DMA((n,))

    tiles = (HS, BLOCK)
    tall = jax.ShapeDtypeStruct((HEADS, *tiles), BF16)
    columns = D // SHARDS
    lo, q, kv, fa, fb, wg = pl.pallas_call(
        kernel,
        out_shape=(
            jax.ShapeDtypeStruct((BLOCK, D), BF16),
            tall,
            jax.ShapeDtypeStruct((HEADS, 2 * HS, BLOCK), BF16),
            jax.ShapeDtypeStruct((HEADS, MANY, BLOCK), BF16),
            jax.ShapeDtypeStruct((HEADS, FEW, BLOCK), BF16),
            jax.ShapeDtypeStruct((columns, HS), F32),
        ),
        in_specs=[any_space] * 9,
        out_specs=(any_space,) * 6,
        scratch_shapes=[
            buf(1, SHARDS * TILES, dtype=jnp.int32), pltpu.SMEM((SHARDS * TILES,), jnp.int32),
            pltpu.SMEM((SHARDS * TILES,), jnp.int32), pltpu.SMEM((KMAX, QB), jnp.int32),
            pltpu.SMEM((QB,), jnp.int32), buf(BLOCK, D), buf(columns, HS, dtype=F32),
            buf(SHARDS, BLOCK, dtype=jnp.int32), buf(2 * SHARDS, BLOCK, dtype=jnp.int32),
            pltpu.SMEM((2 * SHARDS, BLOCK), jnp.int32),
            buf(8, BLOCK, dtype=jnp.int32), pltpu.SMEM((8, BLOCK), jnp.int32),
            buf(BLOCK, 4 * D), buf(BLOCK, D), buf(D, D), buf(TILES, BLOCK, BLOCK),
            buf(HEADS, FEW, BLOCK), buf(HEADS, MANY, BLOCK), buf(HEADS, 3 * HS, BLOCK),
            buf(HEADS, FEW, BLOCK), buf(HEADS, MANY, BLOCK), buf(HEADS, 3 * HS, BLOCK),
            buf(QB, D, BLOCK), buf(QB, *tiles), buf(QB, BLOCK, 2 * HS),
            buf(TILES, FEW, BLOCK), buf(TILES, MANY, BLOCK),
            buf(SLOTS, FEW, BLOCK), buf(SLOTS, MANY, BLOCK),
            buf(SLOTS, FEW, BLOCK), buf(SLOTS, MANY, BLOCK),
            buf(SLOTS, MANY, BLOCK), buf(SLOTS, FEW, BLOCK),
            buf(SLOTS, MANY, BLOCK), buf(SLOTS, FEW, BLOCK),
            buf(SLOTS + 1, *tiles, dtype=F32), buf(SLOTS + 1, MANY, BLOCK, dtype=F32),
            buf(SLOTS + 1, FEW, BLOCK, dtype=F32),
            buf(QB * KMAX + 1, *tiles, dtype=F32), buf(QB * KMAX + 1, *tiles, dtype=F32),
            buf(HEADS, 2 * HS, BLOCK), buf(HEADS, 2 * HS, BLOCK),
            buf(HEADS, MANY, BLOCK), buf(HEADS, FEW, BLOCK), buf(HEADS, *tiles),
            buf(HEADS, 2 * HS, BLOCK), buf(HEADS, *tiles),
            buf(D, HS, dtype=F32), buf(SHARDS, D // SHARDS, HS, dtype=F32),
            buf(NX, NZ, D // SHARDS, HS, dtype=F32),
            buf(NZ, D // SHARDS, HS, dtype=F32), buf(NZ, D // SHARDS, HS, dtype=F32),
            sems(9), sems(2), sems(6), *[sems(HEADS)] * 6,
            sems(7), sems(7), sems(7), sems(7), sems(8), sems(8), *[sems(SHARDS)] * 8,
            *[sems(HEADS)] * 10, sems(NX), sems(NX), sems(NZ), sems(NZ),
        ],
        compiler_params=pltpu.CompilerParams(
            collective_id=0, has_side_effects=True, vmem_limit_bytes=61 << 20
        ),
    )(
        tile_owner.T, source_block, target_block, key_blocks.T, key_count,
        projected, upstream, out_weight, tile_weights,
    )
    layer_out, grad_projected, weight_grad = pl.pallas_call(
        finish,
        out_shape=(
            jax.ShapeDtypeStruct((BLOCK, D), BF16),
            jax.ShapeDtypeStruct((BLOCK, 4 * D), BF16),
            jax.ShapeDtypeStruct((columns, HS), F32),
        ),
        in_specs=[any_space] * 6,
        out_specs=(any_space,) * 3,
        scratch_shapes=[
            buf(BLOCK, D), buf(HEADS, *tiles), buf(HEADS, 2 * HS, BLOCK), buf(HEADS, MANY, BLOCK),
            buf(HEADS, FEW, BLOCK), buf(columns, HS, dtype=F32), buf(BLOCK, 4 * D), sems(12),
        ],
        compiler_params=pltpu.CompilerParams(vmem_limit_bytes=61 << 20),
    )(lo, q, kv, fa, fb, wg)
    return layer_out, grad_projected, weight_grad.T


def solution(mesh):
    in_specs = (
        P(("seq", "head"), None), P(("seq", "head"), None), P(), P("seq", None, None),
        P(), P(), P(), P("seq", None), P("seq"),
    )
    out_specs = (P(("seq", "head"), None), P(("seq", "head"), None), P("head", "seq"))
    return jax.shard_map(body, mesh=mesh, in_specs=in_specs, out_specs=out_specs, check_vma=False)
```

```python
import functools
import math

import jax
import jax.numpy as jnp
from jax import lax
from jax.experimental import pallas as pl
from jax.experimental.pallas import tpu as pltpu
from jax.sharding import PartitionSpec as P

MESH = pl.DeviceIdType.MESH
HEADS = 16
BLOCK = 128
CAP = 3
HS = 48
D = 768
QB = 16
KMAX = 4
TILES = 48
SHARDS = 32
SLOTS = SHARDS * CAP
NX = 4
NZ = 8
F32 = jnp.float32
BF16 = jnp.bfloat16

PREV_SRC, LAST_SRC, PREV_TGT, LAST_TGT, PREV_KEY, LAST_KEY = range(6)
FEW, MANY = 16, 32


def nn(a, b):
    return lax.dot_general(a, b, (((1,), (0,)), ((), ())), preferred_element_type=F32)


def nt(a, b):
    return lax.dot_general(a, b, (((1,), (1,)), ((), ())), preferred_element_type=F32)


def each(start, stop, unroll=1):
    def run(f):
        def step(i, carry):
            f(i)
            return carry

        lax.fori_loop(start, stop, step, 0, unroll=unroll)

    return run


def kernel(
    own_in, sources_in, targets_in, keys_in, counts_in, pj, up, ow, tw,
    lo_out, q_out, r_kv, r_fa, r_fb, wg_out,
    own, sources, targets, keys, counts, lo_v, wg_v,
    own_m, slots_v, slots, chains_v, chains,
    pjv, upv, owv, twv,
    p_fa, p_fb, p_q, f_ta, f_tb, q_t, u_t, g_t, kv,
    part_a, part_b, outg_a, outg_b, arr_a, arr_b, rep_a, rep_b, ret_a, ret_b,
    run_t, run_sa, run_sb, run_k, run_v,
    s_a, s_kv, s_fa, s_fb, s_m, r_a, r_m,
    wg_acc, wg_p, wx_r, wz_p, wz_r,
    ld, tb, out, fas, far, fbs, fbr, qs, qr, rs, rr, ls, lr, bs, br,
    pas, par, pbs, pbr, eas, ear, ebs, ebr,
    as_, ar, ks, kr, has, har, hbs, hbr, ms, mr, xs, xr, zs, zr,
):
    s = lax.axis_index("seq")
    h = lax.axis_index("head")
    z = s // NX
    x = s % NX
    sib = h + 1 - 2 * (h % 2)
    right, left = (h + 2) % HEADS, (h + HEADS - 2) % HEADS
    my_rows = pl.ds(pl.multiple_of(h * HS, 16), HS)
    my_many = pl.ds(pl.multiple_of(h * HS, 16), MANY)
    my_few = pl.ds(pl.multiple_of(h * HS + MANY, 16), FEW)

    def remote(src, dst, send, recv, axis, peer):
        return pltpu.make_async_remote_copy(
            src_ref=src, dst_ref=dst, send_sem=send, recv_sem=recv,
            device_id={axis: peer}, device_id_type=MESH,
        )

    def head_copy(src, dst, send, recv):
        def at(d):
            peer = (h + d) % HEADS
            return remote(src.at[peer], dst.at[h], send.at[d], recv.at[d], "head", peer)

        return at

    def seq_copy(src, dst, send, recv):
        def at(d):
            peer = (s + d) % SHARDS
            return remote(
                src.at[pl.ds(peer * CAP, CAP)], dst.at[pl.ds(s * CAP, CAP)],
                send.at[d], recv.at[d], "seq", peer,
            )

        return at

    c_fa = head_copy(p_fa, f_ta, fas, far)
    c_fb = head_copy(p_fb, f_tb, fbs, fbr)
    c_q = head_copy(p_q, q_t, qs, qr)
    c_a = head_copy(s_a, r_a, as_, ar)
    c_kv = head_copy(s_kv, r_kv, ks, kr)
    c_dfa = head_copy(s_fa, r_fa, has, har)
    c_dfb = head_copy(s_fb, r_fb, hbs, hbr)
    c_m = head_copy(s_m, r_m, ms, mr)
    c_pa = seq_copy(outg_a, arr_a, pas, par)
    c_pb = seq_copy(outg_b, arr_b, pbs, pbr)
    c_ea = seq_copy(rep_a, ret_a, eas, ear)
    c_eb = seq_copy(rep_b, ret_b, ebs, ebr)

    def start_all(copy, n):
        each(1, n)(lambda d: copy(d).start())

    def recv_all(copy, n):
        each(1, n)(lambda d: copy(d).wait_recv())

    def send_all(copy, n):
        each(1, n)(lambda d: copy(d).wait_send())

    half = D // 2
    first, second = pl.ds(0, half), pl.ds(half, half)

    def ring_right(i, lead):
        ref = u_t.at[(h + HEADS - 2 * i) % HEADS, first if lead else second]
        n = 2 * i + 1 - lead
        return remote(ref, ref, rs.at[n], rr.at[n], "head", right)

    def ring_left(i, lead):
        ref = u_t.at[(h + 2 * i) % HEADS, second if lead else first]
        n = 2 * i + 1 - lead
        return remote(ref, ref, ls.at[n], lr.at[n], "head", left)

    def to_sib(k):
        ref = u_t.at[(h + 2 * k) % HEADS]
        return remote(ref, ref, bs.at[k], br.at[k], "head", sib)

    l_up = pltpu.make_async_copy(up, upv, ld.at[0])
    l_pj = pltpu.make_async_copy(pj, pjv, ld.at[1])
    l_tw = pltpu.make_async_copy(tw, twv, ld.at[2])
    l_ow = pltpu.make_async_copy(ow, owv, ld.at[3])
    small = (
        (own_in, own), (sources_in, sources), (targets_in, targets), (keys_in, keys),
        (counts_in, counts),
    )
    l_small = [pltpu.make_async_copy(a, b, ld.at[4 + n]) for n, (a, b) in enumerate(small)]
    l_pj.start()
    l_up.start()
    barrier = pltpu.get_barrier_semaphore()
    for d in range(1, HEADS):
        pl.semaphore_signal(
            barrier, inc=1, device_id={"head": (h + d) % HEADS}, device_id_type=MESH
        )
    for d in range(1, SHARDS):
        pl.semaphore_signal(
            barrier, inc=1, device_id={"seq": (s + d) % SHARDS}, device_id_type=MESH
        )
    for load in (*l_small, l_tw, l_ow):
        load.start()
    l_pj.wait()
    for i in range(HEADS // 2):
        pair = pjv[:, 8 * HS * i : 8 * HS * (i + 1)].T
        for k in range(2):
            p_q[2 * i + k] = pair[4 * HS * k : 4 * HS * k + 3 * HS]
            p_fa[2 * i + k] = pair[4 * HS * k + 3 * HS : 4 * HS * k + 3 * HS + FEW]
            p_fb[2 * i + k] = pair[4 * HS * k + 3 * HS + FEW : 4 * HS * (k + 1)]
    pl.semaphore_wait(barrier, HEADS + SHARDS - 2)

    start_all(c_fa, HEADS)
    start_all(c_fb, HEADS)
    f_ta[h] = p_fa[h]
    f_tb[h] = p_fb[h]
    q_t[h] = p_q[h]
    l_up.wait()
    for i in range(2):
        u_t[h, half * i : half * (i + 1)] = upv[:, half * i : half * (i + 1)].T
    run_t[SLOTS] = jnp.zeros((HS, BLOCK), F32)
    run_sa[SLOTS] = jnp.zeros((MANY, BLOCK), F32)
    run_sb[SLOTS] = jnp.zeros((FEW, BLOCK), F32)
    run_k[QB * KMAX] = jnp.zeros((HS, BLOCK), F32)
    run_v[QB * KMAX] = jnp.zeros((HS, BLOCK), F32)

    def ring_step(i):
        for lead in (1, 0) if i < 4 else (1,):
            for ring in (ring_right, ring_left):
                ring(i - 1, lead).wait_recv()
                if i < 3 or (lead and i < 4):
                    ring(i, lead).start()
        if i < 4:
            to_sib(8 - i).start()
        to_sib(i).start()

    for lead in (1, 0):
        ring_right(0, lead).start()
        ring_left(0, lead).start()
    to_sib(0).start()
    for load in l_small:
        load.wait()
    for n in range(SHARDS):
        own_m[n : n + 1, :TILES] = own[:, TILES * n : TILES * (n + 1)]
    lane = lax.broadcasted_iota(jnp.int32, (SHARDS, BLOCK), 1)
    row = lax.broadcasted_iota(jnp.int32, (SHARDS, BLOCK), 0)
    lane1 = lax.broadcasted_iota(jnp.int32, (1, BLOCK), 1)

    def first_three(same):
        found = []
        for k in range(CAP):
            later = same & (lane > found[-1]) if k else same
            found.append(jnp.min(jnp.where(later, lane, 999), axis=1, keepdims=True))
        return found

    def in_lanes(found, none):
        listed = jnp.where(lane == 0, found[0], jnp.where(lane == 1, found[1], found[2]))
        return jnp.where(listed == 999, none, listed)

    mine = own_m[pl.ds(s, 1), :]
    going = first_three((mine == row) & (lane < TILES))
    coming = first_three((own_m[...] == s) & (lane < TILES))
    slots_v[:SHARDS] = in_lanes(going, -1)
    slots_v[SHARDS:] = in_lanes(coming, -1)
    l_slots = pltpu.make_async_copy(slots_v, slots, tb.at[0])
    l_slots.start()
    def slot_target(n, k):
        tile = slots[SHARDS + n, k]
        return tile, targets[TILES * n + jnp.maximum(tile, 0)]

    def chain(outer, inner, label, none, prev_row, last_row):
        def gather(i, labels):
            for j in range(inner):
                labels = jnp.where(lane1 == inner * i + j, label(i, j), labels)
            return labels

        labels = lax.fori_loop(0, outer, gather, jnp.full((1, BLOCK), -2, jnp.int32))

        def link(i, carry):
            prev, last = carry
            for j in range(inner):
                at, here = inner * i + j, label(i, j)
                prev = jnp.where((labels == here) & (lane1 > at), at, prev)
                last = jnp.where(lane1 == here, at, last)
            return prev, last

        empty = jnp.full((1, BLOCK), none, jnp.int32)
        prev, last = lax.fori_loop(0, outer, link, (empty, empty))
        chains_v[prev_row : prev_row + 1] = prev
        chains_v[last_row : last_row + 1] = last

    def source(d, k):
        tile = slots[(s + SHARDS - d) % SHARDS, k]
        return jnp.where(tile < 0, -1, sources[TILES * s + jnp.maximum(tile, 0)])

    def target(i, j):
        tile, at = slot_target(i, j)
        return jnp.where(tile < 0, -1, at)

    def key(i, j):
        return keys[j, (h + 1 + i) % QB]

    l_slots.wait()
    l_tw.wait()

    def products(f_t, part, outg):
        @each(0, TILES, 8)
        def _(t):
            part[t] = nt(f_t[sources[TILES * s + t]], twv[t]).astype(BF16)

        @each(0, SHARDS, 4)
        def _(n):
            for k in range(CAP):
                outg[CAP * n + k] = part[jnp.maximum(slots[n, k], 0)]

    own_slots = pl.ds(s * CAP, CAP)
    recv_all(c_fa, HEADS)
    products(f_ta, part_a, outg_a)
    start_all(c_pa, SHARDS)
    recv_all(c_fb, HEADS)
    ring_step(1)
    products(f_tb, part_b, outg_b)
    start_all(c_pb, SHARDS)
    each(1, 4)(lambda d: c_q(d).start())
    arr_a[own_slots] = outg_a[own_slots]
    arr_b[own_slots] = outg_b[own_slots]
    chain(SHARDS, CAP, source, SLOTS, PREV_SRC, LAST_SRC)
    chain(QB, KMAX, key, QB * KMAX, PREV_KEY, LAST_KEY)
    ring_step(2)
    each(4, 8)(lambda d: c_q(d).start())
    chain(SHARDS, CAP, target, SLOTS, PREV_TGT, LAST_TGT)
    l_chains = pltpu.make_async_copy(chains_v, chains, tb.at[1])
    l_chains.start()
    ring_step(3)
    each(8, HEADS)(lambda d: c_q(d).start())
    ring_step(4)
    each(0, 8)(lambda k: to_sib(k).wait_recv())
    l_chains.wait()

    def replies(rep, ret, rows):
        @each(0, SHARDS, 4)
        def _(n):
            for k in range(CAP):
                rep[CAP * n + k] = u_t[slot_target(n, k)[1], rows]

        ret[own_slots] = rep[own_slots]

    replies(rep_a, ret_a, my_many)
    start_all(c_ea, SHARDS)
    replies(rep_b, ret_b, my_few)
    start_all(c_eb, SHARDS)

    l_ow.wait()

    @each(0, QB, 2)
    def _(b):
        g_t[b] = nn(owv[my_rows], u_t[b]).astype(BF16)

    recv_all(c_pa, SHARDS)
    recv_all(c_pb, SHARDS)

    @each(0, SLOTS, 8)
    def _(p):
        before = run_t[chains[PREV_TGT, p]]
        run_t[p, :FEW] = arr_a[p].astype(F32) + before[:FEW]
        run_t[p, FEW:] = arr_b[p].astype(F32) + before[FEW:]

    @each(1, HEADS)
    def _(d):
        b = (h + d) % HEADS
        s_m[b] = run_t[chains[LAST_TGT, b]].astype(BF16)
        c_m(d).start()

    r_m[h] = run_t[chains[LAST_TGT, h]].astype(BF16)

    for copy in (c_fa, c_fb):
        send_all(copy, HEADS)
    for copy in (c_pa, c_pb):
        send_all(copy, SHARDS)
    for i in range(4):
        for lead in (1, 0) if i < 3 else (1,):
            ring_right(i, lead).wait_send()
            ring_left(i, lead).wait_send()
    each(0, 8)(lambda k: to_sib(k).wait_send())
    recv_all(c_q, HEADS)

    @each(0, QB, 2)
    def _(b):
        kv[b] = q_t[b, HS:].T

    scale = HS ** (-0.5)
    pad = jnp.zeros((HS, BLOCK), BF16)

    def attend(i):
        r = (h + 1 + i) % QB
        q = q_t[r, :HS]
        g = g_t[r]
        blocks = [keys[j, r] for j in range(KMAX)]
        count = counts[r]
        qg = jnp.concatenate(
            [jnp.concatenate([q, pad], axis=1), jnp.concatenate([pad, g], axis=1)], axis=0
        )
        both = [nn(kv[blocks[j]], qg) for j in range(KMAX)]
        scores = [
            both[j][:, :BLOCK] * scale + jnp.where(j < count, 0.0, -jnp.inf).astype(F32)
            for j in range(KMAX)
        ]
        grad_prob = [both[j][:, BLOCK:] for j in range(KMAX)]
        top = functools.reduce(
            jnp.maximum, [jnp.max(sc, axis=0, keepdims=True) for sc in scores]
        )
        expo = [jnp.exp(sc - top) for sc in scores]
        total = sum(jnp.sum(e, axis=0, keepdims=True) for e in expo)
        inverse = 1.0 / total
        prob = [e * inverse for e in expo]
        delta = sum(
            jnp.sum(a * b, axis=0, keepdims=True) for a, b in zip(prob, grad_prob)
        )
        prob_b = jnp.concatenate([a.astype(BF16) for a in prob], axis=0)
        dscore = jnp.concatenate(
            [(a * (b - delta) * scale).astype(BF16) for a, b in zip(prob, grad_prob)], axis=0
        )
        keys_t = jnp.concatenate([q_t[b, HS : 2 * HS] for b in blocks], axis=1)
        values_t = jnp.concatenate([q_t[b, 2 * HS :] for b in blocks], axis=1)
        s_a[r, :HS] = nn(values_t, prob_b).astype(BF16)
        s_a[r, HS:] = nn(keys_t, dscore).astype(BF16)
        term_k = nt(q, dscore)
        term_v = nt(g, prob_b)
        for j in range(KMAX):
            before = chains[PREV_KEY, KMAX * i + j]
            lanes = slice(BLOCK * j, BLOCK * (j + 1))
            run_k[KMAX * i + j] = term_k[:, lanes] + run_k[before]
            run_v[KMAX * i + j] = term_v[:, lanes] + run_v[before]

    @each(0, QB // 4)
    def _(g):
        for j in range(4):
            attend(4 * g + j)
        for j in range(3):
            c_a(4 * g + j + 1).start()

        @pl.when(g < QB // 4 - 1)
        def _():
            c_a(4 * g + 4).start()

    r_a[h] = s_a[h]

    @each(1, HEADS)
    def _(d):
        b = (h + d) % HEADS
        last = chains[LAST_KEY, b]
        s_kv[b, :HS] = run_k[last].astype(BF16)
        s_kv[b, HS:] = run_v[last].astype(BF16)
        c_kv(d).start()

    last_own = chains[LAST_KEY, h]
    s_kv[h, :HS] = run_k[last_own].astype(BF16)
    s_kv[h, HS:] = run_v[last_own].astype(BF16)
    o_kv = pltpu.make_async_copy(s_kv.at[h], r_kv.at[h], out.at[0])
    o_kv.start()

    wg_acc[...] = nt(u_t[0], s_a[0, :HS])

    @each(1, QB)
    def _(b):
        wg_acc[...] += nt(u_t[b], s_a[b, :HS])

    columns = D // SHARDS
    for n in range(SHARDS):
        wg_p[(n % NX) * NZ + n // NX] = wg_acc[columns * n : columns * (n + 1)]

    def c_x(d):
        to = (x + d) % NX
        return remote(
            wg_p.at[pl.ds(to * NZ, NZ)], wx_r.at[x], xs.at[d], xr.at[d], "seq", z * NX + to
        )

    def c_z(d):
        to = (z + d) % NZ
        return remote(wz_p.at[to], wz_r.at[z], zs.at[d], zr.at[d], "seq", to * NX + x)

    start_all(c_x, NX)
    wx_r[x] = wg_p[pl.ds(x * NZ, NZ)]

    group = 4

    def back(copy, ret, run, sent):
        def some(g, first):
            for j in range(first, group):
                copy(group * g + j).wait_recv()
            for j in range(group):
                d = group * g + j
                n = (s + SHARDS - d) % SHARDS
                for k in range(CAP):
                    q = CAP * d + k
                    term = nn(ret[CAP * n + k], twv[jnp.maximum(slots[n, k], 0)])
                    run[q] = term + run[chains[PREV_SRC, q]]

        some(0, 1)
        each(1, SHARDS // group)(lambda g: some(g, 0))

        @each(0, QB, 4)
        def _(b):
            sent[b] = run[chains[LAST_SRC, b]].astype(BF16)

    back(c_ea, ret_a, run_sa, s_fa)
    start_all(c_dfa, HEADS)
    o_fa = pltpu.make_async_copy(s_fa.at[h], r_fa.at[h], out.at[1])
    o_fa.start()
    back(c_eb, ret_b, run_sb, s_fb)
    start_all(c_dfb, HEADS)
    o_fb = pltpu.make_async_copy(s_fb.at[h], r_fb.at[h], out.at[5])
    o_fb.start()
    recv_all(c_x, NX)
    wz_p[...] = wx_r[0] + wx_r[1] + wx_r[2] + wx_r[3]
    wz_r[z] = wz_p[z]
    start_all(c_z, NZ)

    recv_all(c_a, HEADS)
    o_q = pltpu.make_async_copy(r_a.at[:, pl.ds(HS, HS)], q_out, out.at[3])
    o_q.start()
    recv_all(c_m, HEADS)
    per = HEADS // 2
    acc = jnp.zeros((BLOCK, D), F32)
    for i in range(2):
        wide = jnp.concatenate([r_a[per * i + k, :HS] for k in range(per)], axis=0).T
        acc = acc + nn(wide, owv[half * i : half * (i + 1)])
    mixed = [
        jnp.concatenate([r_m[per * i + k] for k in range(per)], axis=0).T for i in range(2)
    ]
    lo_v[...] = (acc + jnp.concatenate(mixed, axis=1).astype(F32)).astype(BF16)
    o_lo = pltpu.make_async_copy(lo_v, lo_out, out.at[4])
    o_lo.start()
    recv_all(c_z, NZ)
    total = wz_r[0]
    for n in range(1, NZ):
        total = total + wz_r[n]
    wg_v[...] = total * (1.0 / math.sqrt(SHARDS * QB * BLOCK))
    o_wg = pltpu.make_async_copy(wg_v, wg_out, out.at[2])
    o_wg.start()

    for copy in (c_q, c_m, c_a, c_kv):
        send_all(copy, HEADS)
    for copy in (c_ea, c_eb):
        send_all(copy, SHARDS)
    send_all(c_x, NX)
    recv_all(c_kv, HEADS)
    recv_all(c_dfa, HEADS)
    recv_all(c_dfb, HEADS)
    for copy in (o_kv, o_fa, o_fb, o_wg, o_q, o_lo):
        copy.wait()

    for copy in (c_dfa, c_dfb):
        send_all(copy, HEADS)
    send_all(c_z, NZ)


def finish(
    lo, q, kv, fa, fb, wg, lo_out, gp_out, wg_out,
    lo_v, q_v, kv_v, fa_v, fb_v, wg_v, gp_v, sem,
):
    loads = [
        pltpu.make_async_copy(a, b, sem.at[n])
        for n, (a, b) in enumerate(
            ((lo, lo_v), (wg, wg_v), (q, q_v), (kv, kv_v), (fa, fa_v), (fb, fb_v))
        )
    ]
    for copy in loads:
        copy.start()
    stores = [
        pltpu.make_async_copy(a, b, sem.at[10 + n])
        for n, (a, b) in enumerate(((lo_v, lo_out), (wg_v, wg_out)))
    ]
    for copy in loads:
        copy.wait()
    for copy in stores:
        copy.start()
    wide = 8 * HS
    for i in range(HEADS // 2):
        rows = []
        for n in (2 * i, 2 * i + 1):
            rows += [q_v[n], kv_v[n], fa_v[n], fb_v[n]]
        lanes = pl.ds(wide * i, wide)
        gp_v[:, lanes] = jnp.concatenate(rows, axis=0).T
        if i % 2:
            lanes = pl.ds(wide * (i - 1), 2 * wide)
            stores.append(
                pltpu.make_async_copy(gp_v.at[:, lanes], gp_out.at[:, lanes], sem.at[6 + i // 2])
            )
            stores[-1].start()
    for copy in stores:
        copy.wait()


def body(
    projected, upstream, out_weight, tile_weights, tile_owner,
    source_block, target_block, key_blocks, key_count,
):
    any_space = pl.BlockSpec(memory_space=pl.ANY)

    def buf(*shape, dtype=BF16):
        return pltpu.VMEM(shape, dtype)

    def sems(n):
        return pltpu.SemaphoreType.DMA((n,))

    tiles = (HS, BLOCK)
    tall = jax.ShapeDtypeStruct((HEADS, *tiles), BF16)
    columns = D // SHARDS
    lo, q, kv, fa, fb, wg = pl.pallas_call(
        kernel,
        out_shape=(
            jax.ShapeDtypeStruct((BLOCK, D), BF16),
            tall,
            jax.ShapeDtypeStruct((HEADS, 2 * HS, BLOCK), BF16),
            jax.ShapeDtypeStruct((HEADS, MANY, BLOCK), BF16),
            jax.ShapeDtypeStruct((HEADS, FEW, BLOCK), BF16),
            jax.ShapeDtypeStruct((columns, HS), F32),
        ),
        in_specs=[any_space] * 9,
        out_specs=(any_space,) * 6,
        scratch_shapes=[
            buf(1, SHARDS * TILES, dtype=jnp.int32), pltpu.SMEM((SHARDS * TILES,), jnp.int32),
            pltpu.SMEM((SHARDS * TILES,), jnp.int32), pltpu.SMEM((KMAX, QB), jnp.int32),
            pltpu.SMEM((QB,), jnp.int32), buf(BLOCK, D), buf(columns, HS, dtype=F32),
            buf(SHARDS, BLOCK, dtype=jnp.int32), buf(2 * SHARDS, BLOCK, dtype=jnp.int32),
            pltpu.SMEM((2 * SHARDS, BLOCK), jnp.int32),
            buf(8, BLOCK, dtype=jnp.int32), pltpu.SMEM((8, BLOCK), jnp.int32),
            buf(BLOCK, 4 * D), buf(BLOCK, D), buf(D, D), buf(TILES, BLOCK, BLOCK),
            buf(HEADS, FEW, BLOCK), buf(HEADS, MANY, BLOCK), buf(HEADS, 3 * HS, BLOCK),
            buf(HEADS, FEW, BLOCK), buf(HEADS, MANY, BLOCK), buf(HEADS, 3 * HS, BLOCK),
            buf(QB, D, BLOCK), buf(QB, *tiles), buf(QB, BLOCK, 2 * HS),
            buf(TILES, FEW, BLOCK), buf(TILES, MANY, BLOCK),
            buf(SLOTS, FEW, BLOCK), buf(SLOTS, MANY, BLOCK),
            buf(SLOTS, FEW, BLOCK), buf(SLOTS, MANY, BLOCK),
            buf(SLOTS, MANY, BLOCK), buf(SLOTS, FEW, BLOCK),
            buf(SLOTS, MANY, BLOCK), buf(SLOTS, FEW, BLOCK),
            buf(SLOTS + 1, *tiles, dtype=F32), buf(SLOTS + 1, MANY, BLOCK, dtype=F32),
            buf(SLOTS + 1, FEW, BLOCK, dtype=F32),
            buf(QB * KMAX + 1, *tiles, dtype=F32), buf(QB * KMAX + 1, *tiles, dtype=F32),
            buf(HEADS, 2 * HS, BLOCK), buf(HEADS, 2 * HS, BLOCK),
            buf(HEADS, MANY, BLOCK), buf(HEADS, FEW, BLOCK), buf(HEADS, *tiles),
            buf(HEADS, 2 * HS, BLOCK), buf(HEADS, *tiles),
            buf(D, HS, dtype=F32), buf(SHARDS, D // SHARDS, HS, dtype=F32),
            buf(NX, NZ, D // SHARDS, HS, dtype=F32),
            buf(NZ, D // SHARDS, HS, dtype=F32), buf(NZ, D // SHARDS, HS, dtype=F32),
            sems(9), sems(2), sems(6), *[sems(HEADS)] * 6,
            sems(7), sems(7), sems(7), sems(7), sems(8), sems(8), *[sems(SHARDS)] * 8,
            *[sems(HEADS)] * 10, sems(NX), sems(NX), sems(NZ), sems(NZ),
        ],
        compiler_params=pltpu.CompilerParams(
            collective_id=0, has_side_effects=True, vmem_limit_bytes=61 << 20
        ),
    )(
        tile_owner.T, source_block, target_block, key_blocks.T, key_count,
        projected, upstream, out_weight, tile_weights,
    )
    layer_out, grad_projected, weight_grad = pl.pallas_call(
        finish,
        out_shape=(
            jax.ShapeDtypeStruct((BLOCK, D), BF16),
            jax.ShapeDtypeStruct((BLOCK, 4 * D), BF16),
            jax.ShapeDtypeStruct((columns, HS), F32),
        ),
        in_specs=[any_space] * 6,
        out_specs=(any_space,) * 3,
        scratch_shapes=[
            buf(BLOCK, D), buf(HEADS, *tiles), buf(HEADS, 2 * HS, BLOCK), buf(HEADS, MANY, BLOCK),
            buf(HEADS, FEW, BLOCK), buf(columns, HS, dtype=F32), buf(BLOCK, 4 * D), sems(12),
        ],
        compiler_params=pltpu.CompilerParams(vmem_limit_bytes=61 << 20),
    )(lo, q, kv, fa, fb, wg)
    return layer_out, grad_projected, weight_grad.T


def solution(mesh):
    in_specs = (
        P(("seq", "head"), None), P(("seq", "head"), None), P(), P("seq", None, None),
        P(), P(), P(), P("seq", None), P("seq"),
    )
    out_specs = (P(("seq", "head"), None), P(("seq", "head"), None), P("head", "seq"))
    return jax.shard_map(body, mesh=mesh, in_specs=in_specs, out_specs=out_specs, check_vma=False)
```

```python
import functools
import math

import jax
import jax.numpy as jnp
from jax import lax
from jax.experimental import pallas as pl
from jax.experimental.pallas import tpu as pltpu
from jax.sharding import PartitionSpec as P

MESH = pl.DeviceIdType.MESH
HEADS = 16
BLOCK = 128
CAP = 3
HS = 48
D = 768
QB = 16
KMAX = 4
TILES = 48
SHARDS = 32
SLOTS = SHARDS * CAP
NX = 4
NZ = 8
F32 = jnp.float32
BF16 = jnp.bfloat16

PREV_SRC, LAST_SRC, PREV_TGT, LAST_TGT, PREV_KEY, LAST_KEY = range(6)
FEW, MANY = 16, 32


def nn(a, b):
    return lax.dot_general(a, b, (((1,), (0,)), ((), ())), preferred_element_type=F32)


def nt(a, b):
    return lax.dot_general(a, b, (((1,), (1,)), ((), ())), preferred_element_type=F32)


def each(start, stop, unroll=1):
    def run(f):
        def step(i, carry):
            f(i)
            return carry

        lax.fori_loop(start, stop, step, 0, unroll=unroll)

    return run


def kernel(
    own_in, sources_in, targets_in, keys_in, counts_in, pj, up, ow, tw,
    lo_out, q_out, r_kv, r_fa, r_fb, wg_out,
    own, sources, targets, keys, counts, lo_v, wg_v,
    own_m, slots_v, slots, chains_v, chains,
    pjv, upv, owv, twv,
    p_fa, p_fb, p_q, f_ta, f_tb, q_t, u_t, g_t, kv,
    part_a, part_b, outg_a, outg_b, arr_a, arr_b, rep_a, rep_b, ret_a, ret_b,
    run_t, run_sa, run_sb, run_k, run_v,
    s_a, s_kv, s_fa, s_fb, s_m, r_a, r_m,
    wg_acc, wg_p, wx_r, wz_p, wz_r,
    ld, tb, out, fas, far, fbs, fbr, qs, qr, rs, rr, ls, lr, bs, br,
    pas, par, pbs, pbr, eas, ear, ebs, ebr,
    as_, ar, ks, kr, has, har, hbs, hbr, ms, mr, xs, xr, zs, zr,
):
    s = lax.axis_index("seq")
    h = lax.axis_index("head")
    z = s // NX
    x = s % NX
    sib = h + 1 - 2 * (h % 2)
    right, left = (h + 2) % HEADS, (h + HEADS - 2) % HEADS
    my_rows = pl.ds(pl.multiple_of(h * HS, 16), HS)
    my_many = pl.ds(pl.multiple_of(h * HS, 16), MANY)
    my_few = pl.ds(pl.multiple_of(h * HS + MANY, 16), FEW)

    def remote(src, dst, send, recv, axis, peer):
        return pltpu.make_async_remote_copy(
            src_ref=src, dst_ref=dst, send_sem=send, recv_sem=recv,
            device_id={axis: peer}, device_id_type=MESH,
        )

    def head_copy(src, dst, send, recv):
        def at(d):
            peer = (h + d) % HEADS
            return remote(src.at[peer], dst.at[h], send.at[d], recv.at[d], "head", peer)

        return at

    def seq_copy(src, dst, send, recv):
        def at(d):
            peer = (s + d) % SHARDS
            return remote(
                src.at[pl.ds(peer * CAP, CAP)], dst.at[pl.ds(s * CAP, CAP)],
                send.at[d], recv.at[d], "seq", peer,
            )

        return at

    c_fa = head_copy(p_fa, f_ta, fas, far)
    c_fb = head_copy(p_fb, f_tb, fbs, fbr)
    c_q = head_copy(p_q, q_t, qs, qr)
    c_a = head_copy(s_a, r_a, as_, ar)
    c_kv = head_copy(s_kv, r_kv, ks, kr)
    c_dfa = head_copy(s_fa, r_fa, has, har)
    c_dfb = head_copy(s_fb, r_fb, hbs, hbr)
    c_m = head_copy(s_m, r_m, ms, mr)
    c_pa = seq_copy(outg_a, arr_a, pas, par)
    c_pb = seq_copy(outg_b, arr_b, pbs, pbr)
    c_ea = seq_copy(rep_a, ret_a, eas, ear)
    c_eb = seq_copy(rep_b, ret_b, ebs, ebr)

    def start_all(copy, n):
        each(1, n)(lambda d: copy(d).start())

    def recv_all(copy, n):
        each(1, n)(lambda d: copy(d).wait_recv())

    def send_all(copy, n):
        each(1, n)(lambda d: copy(d).wait_send())

    half = D // 2
    first, second = pl.ds(0, half), pl.ds(half, half)

    def ring_right(i, lead):
        ref = u_t.at[(h + HEADS - 2 * i) % HEADS, first if lead else second]
        n = 2 * i + 1 - lead
        return remote(ref, ref, rs.at[n], rr.at[n], "head", right)

    def ring_left(i, lead):
        ref = u_t.at[(h + 2 * i) % HEADS, second if lead else first]
        n = 2 * i + 1 - lead
        return remote(ref, ref, ls.at[n], lr.at[n], "head", left)

    def to_sib(k):
        ref = u_t.at[(h + 2 * k) % HEADS]
        return remote(ref, ref, bs.at[k], br.at[k], "head", sib)

    l_up = pltpu.make_async_copy(up, upv, ld.at[0])
    l_pj = pltpu.make_async_copy(pj, pjv, ld.at[1])
    l_tw = pltpu.make_async_copy(tw, twv, ld.at[2])
    l_ow = pltpu.make_async_copy(ow, owv, ld.at[3])
    small = (
        (own_in, own), (sources_in, sources), (targets_in, targets), (keys_in, keys),
        (counts_in, counts),
    )
    l_small = [pltpu.make_async_copy(a, b, ld.at[4 + n]) for n, (a, b) in enumerate(small)]
    l_pj.start()
    l_up.start()
    barrier = pltpu.get_barrier_semaphore()
    for d in range(1, HEADS):
        pl.semaphore_signal(
            barrier, inc=1, device_id={"head": (h + d) % HEADS}, device_id_type=MESH
        )
    for d in range(1, SHARDS):
        pl.semaphore_signal(
            barrier, inc=1, device_id={"seq": (s + d) % SHARDS}, device_id_type=MESH
        )
    for load in (*l_small, l_tw, l_ow):
        load.start()
    l_pj.wait()
    for i in range(HEADS // 2):
        pair = pjv[:, 8 * HS * i : 8 * HS * (i + 1)].T
        for k in range(2):
            p_q[2 * i + k] = pair[4 * HS * k : 4 * HS * k + 3 * HS]
            p_fa[2 * i + k] = pair[4 * HS * k + 3 * HS : 4 * HS * k + 3 * HS + FEW]
            p_fb[2 * i + k] = pair[4 * HS * k + 3 * HS + FEW : 4 * HS * (k + 1)]
    pl.semaphore_wait(barrier, HEADS + SHARDS - 2)

    start_all(c_fa, HEADS)
    start_all(c_fb, HEADS)
    f_ta[h] = p_fa[h]
    f_tb[h] = p_fb[h]
    q_t[h] = p_q[h]
    l_up.wait()
    for i in range(2):
        u_t[h, half * i : half * (i + 1)] = upv[:, half * i : half * (i + 1)].T
    run_t[SLOTS] = jnp.zeros((HS, BLOCK), F32)
    run_sa[SLOTS] = jnp.zeros((MANY, BLOCK), F32)
    run_sb[SLOTS] = jnp.zeros((FEW, BLOCK), F32)
    run_k[QB * KMAX] = jnp.zeros((HS, BLOCK), F32)
    run_v[QB * KMAX] = jnp.zeros((HS, BLOCK), F32)

    def ring_step(i):
        for lead in (1, 0) if i < 4 else (1,):
            for ring in (ring_right, ring_left):
                ring(i - 1, lead).wait_recv()
                if i < 3 or (lead and i < 4):
                    ring(i, lead).start()
        if i < 4:
            to_sib(8 - i).start()
        to_sib(i).start()

    for lead in (1, 0):
        ring_right(0, lead).start()
        ring_left(0, lead).start()
    to_sib(0).start()
    for load in l_small:
        load.wait()
    for n in range(SHARDS):
        own_m[n : n + 1, :TILES] = own[:, TILES * n : TILES * (n + 1)]
    lane = lax.broadcasted_iota(jnp.int32, (SHARDS, BLOCK), 1)
    row = lax.broadcasted_iota(jnp.int32, (SHARDS, BLOCK), 0)
    lane1 = lax.broadcasted_iota(jnp.int32, (1, BLOCK), 1)

    def first_three(same):
        found = []
        for k in range(CAP):
            later = same & (lane > found[-1]) if k else same
            found.append(jnp.min(jnp.where(later, lane, 999), axis=1, keepdims=True))
        return found

    def in_lanes(found, none):
        listed = jnp.where(lane == 0, found[0], jnp.where(lane == 1, found[1], found[2]))
        return jnp.where(listed == 999, none, listed)

    mine = own_m[pl.ds(s, 1), :]
    going = first_three((mine == row) & (lane < TILES))
    coming = first_three((own_m[...] == s) & (lane < TILES))
    slots_v[:SHARDS] = in_lanes(going, -1)
    slots_v[SHARDS:] = in_lanes(coming, -1)
    l_slots = pltpu.make_async_copy(slots_v, slots, tb.at[0])
    l_slots.start()
    def slot_target(n, k):
        tile = slots[SHARDS + n, k]
        return tile, targets[TILES * n + jnp.maximum(tile, 0)]

    def chain(outer, inner, label, none, prev_row, last_row):
        def gather(i, labels):
            for j in range(inner):
                labels = jnp.where(lane1 == inner * i + j, label(i, j), labels)
            return labels

        labels = lax.fori_loop(0, outer, gather, jnp.full((1, BLOCK), -2, jnp.int32))

        def link(i, carry):
            prev, last = carry
            for j in range(inner):
                at, here = inner * i + j, label(i, j)
                prev = jnp.where((labels == here) & (lane1 > at), at, prev)
                last = jnp.where(lane1 == here, at, last)
            return prev, last

        empty = jnp.full((1, BLOCK), none, jnp.int32)
        prev, last = lax.fori_loop(0, outer, link, (empty, empty))
        chains_v[prev_row : prev_row + 1] = prev
        chains_v[last_row : last_row + 1] = last

    def source(d, k):
        tile = slots[(s + SHARDS - d) % SHARDS, k]
        return jnp.where(tile < 0, -1, sources[TILES * s + jnp.maximum(tile, 0)])

    def target(i, j):
        tile, at = slot_target(i, j)
        return jnp.where(tile < 0, -1, at)

    def key(i, j):
        return keys[j, (h + 1 + i) % QB]

    l_slots.wait()
    l_tw.wait()

    def products(f_t, part, outg):
        @each(0, TILES, 8)
        def _(t):
            part[t] = nt(f_t[sources[TILES * s + t]], twv[t]).astype(BF16)

        @each(0, SHARDS, 4)
        def _(n):
            for k in range(CAP):
                outg[CAP * n + k] = part[jnp.maximum(slots[n, k], 0)]

    own_slots = pl.ds(s * CAP, CAP)
    recv_all(c_fa, HEADS)
    products(f_ta, part_a, outg_a)
    start_all(c_pa, SHARDS)
    recv_all(c_fb, HEADS)
    ring_step(1)
    products(f_tb, part_b, outg_b)
    start_all(c_pb, SHARDS)
    each(1, 4)(lambda d: c_q(d).start())
    arr_a[own_slots] = outg_a[own_slots]
    arr_b[own_slots] = outg_b[own_slots]
    ring_step(2)
    each(4, 8)(lambda d: c_q(d).start())
    chain(SHARDS, CAP, source, SLOTS, PREV_SRC, LAST_SRC)
    chain(QB, KMAX, key, QB * KMAX, PREV_KEY, LAST_KEY)
    chain(SHARDS, CAP, target, SLOTS, PREV_TGT, LAST_TGT)
    l_chains = pltpu.make_async_copy(chains_v, chains, tb.at[1])
    l_chains.start()
    ring_step(3)
    each(8, HEADS)(lambda d: c_q(d).start())
    ring_step(4)
    each(0, 8)(lambda k: to_sib(k).wait_recv())
    l_chains.wait()

    def replies(rep, ret, rows):
        @each(0, SHARDS, 4)
        def _(n):
            for k in range(CAP):
                rep[CAP * n + k] = u_t[slot_target(n, k)[1], rows]

        ret[own_slots] = rep[own_slots]

    replies(rep_a, ret_a, my_many)
    start_all(c_ea, SHARDS)
    replies(rep_b, ret_b, my_few)
    start_all(c_eb, SHARDS)

    l_ow.wait()

    @each(0, QB, 2)
    def _(b):
        g_t[b] = nn(owv[my_rows], u_t[b]).astype(BF16)

    recv_all(c_pa, SHARDS)
    recv_all(c_pb, SHARDS)

    @each(0, SLOTS, 8)
    def _(p):
        before = run_t[chains[PREV_TGT, p]]
        run_t[p, :FEW] = arr_a[p].astype(F32) + before[:FEW]
        run_t[p, FEW:] = arr_b[p].astype(F32) + before[FEW:]

    @each(1, HEADS)
    def _(d):
        b = (h + d) % HEADS
        s_m[b] = run_t[chains[LAST_TGT, b]].astype(BF16)
        c_m(d).start()

    r_m[h] = run_t[chains[LAST_TGT, h]].astype(BF16)

    for copy in (c_fa, c_fb):
        send_all(copy, HEADS)
    for copy in (c_pa, c_pb):
        send_all(copy, SHARDS)
    for i in range(4):
        for lead in (1, 0) if i < 3 else (1,):
            ring_right(i, lead).wait_send()
            ring_left(i, lead).wait_send()
    each(0, 8)(lambda k: to_sib(k).wait_send())
    recv_all(c_q, HEADS)

    @each(0, QB, 2)
    def _(b):
        kv[b] = q_t[b, HS:].T

    scale = HS ** (-0.5)
    pad = jnp.zeros((HS, BLOCK), BF16)

    def attend(i):
        r = (h + 1 + i) % QB
        q = q_t[r, :HS]
        g = g_t[r]
        blocks = [keys[j, r] for j in range(KMAX)]
        count = counts[r]
        qg = jnp.concatenate(
            [jnp.concatenate([q, pad], axis=1), jnp.concatenate([pad, g], axis=1)], axis=0
        )
        both = [nn(kv[blocks[j]], qg) for j in range(KMAX)]
        scores = [
            both[j][:, :BLOCK] * scale + jnp.where(j < count, 0.0, -jnp.inf).astype(F32)
            for j in range(KMAX)
        ]
        grad_prob = [both[j][:, BLOCK:] for j in range(KMAX)]
        top = functools.reduce(
            jnp.maximum, [jnp.max(sc, axis=0, keepdims=True) for sc in scores]
        )
        expo = [jnp.exp(sc - top) for sc in scores]
        total = sum(jnp.sum(e, axis=0, keepdims=True) for e in expo)
        inverse = 1.0 / total
        prob = [e * inverse for e in expo]
        delta = sum(
            jnp.sum(a * b, axis=0, keepdims=True) for a, b in zip(prob, grad_prob)
        )
        prob_b = jnp.concatenate([a.astype(BF16) for a in prob], axis=0)
        dscore = jnp.concatenate(
            [(a * (b - delta) * scale).astype(BF16) for a, b in zip(prob, grad_prob)], axis=0
        )
        keys_t = jnp.concatenate([q_t[b, HS : 2 * HS] for b in blocks], axis=1)
        values_t = jnp.concatenate([q_t[b, 2 * HS :] for b in blocks], axis=1)
        s_a[r, :HS] = nn(values_t, prob_b).astype(BF16)
        s_a[r, HS:] = nn(keys_t, dscore).astype(BF16)
        term_k = nt(q, dscore)
        term_v = nt(g, prob_b)
        for j in range(KMAX):
            before = chains[PREV_KEY, KMAX * i + j]
            lanes = slice(BLOCK * j, BLOCK * (j + 1))
            run_k[KMAX * i + j] = term_k[:, lanes] + run_k[before]
            run_v[KMAX * i + j] = term_v[:, lanes] + run_v[before]

    @each(0, QB // 4)
    def _(g):
        for j in range(4):
            attend(4 * g + j)
        for j in range(3):
            c_a(4 * g + j + 1).start()

        @pl.when(g < QB // 4 - 1)
        def _():
            c_a(4 * g + 4).start()

    r_a[h] = s_a[h]

    @each(1, HEADS)
    def _(d):
        b = (h + d) % HEADS
        last = chains[LAST_KEY, b]
        s_kv[b, :HS] = run_k[last].astype(BF16)
        s_kv[b, HS:] = run_v[last].astype(BF16)
        c_kv(d).start()

    last_own = chains[LAST_KEY, h]
    s_kv[h, :HS] = run_k[last_own].astype(BF16)
    s_kv[h, HS:] = run_v[last_own].astype(BF16)
    o_kv = pltpu.make_async_copy(s_kv.at[h], r_kv.at[h], out.at[0])
    o_kv.start()

    wg_acc[...] = nt(u_t[0], s_a[0, :HS])

    @each(1, QB)
    def _(b):
        wg_acc[...] += nt(u_t[b], s_a[b, :HS])

    columns = D // SHARDS
    for n in range(SHARDS):
        wg_p[(n % NX) * NZ + n // NX] = wg_acc[columns * n : columns * (n + 1)]

    def c_x(d):
        to = (x + d) % NX
        return remote(
            wg_p.at[pl.ds(to * NZ, NZ)], wx_r.at[x], xs.at[d], xr.at[d], "seq", z * NX + to
        )

    def c_z(d):
        to = (z + d) % NZ
        return remote(wz_p.at[to], wz_r.at[z], zs.at[d], zr.at[d], "seq", to * NX + x)

    start_all(c_x, NX)
    wx_r[x] = wg_p[pl.ds(x * NZ, NZ)]

    group = 4

    def back(copy, ret, run, sent):
        def some(g, first):
            for j in range(first, group):
                copy(group * g + j).wait_recv()
            for j in range(group):
                d = group * g + j
                n = (s + SHARDS - d) % SHARDS
                for k in range(CAP):
                    q = CAP * d + k
                    term = nn(ret[CAP * n + k], twv[jnp.maximum(slots[n, k], 0)])
                    run[q] = term + run[chains[PREV_SRC, q]]

        some(0, 1)
        each(1, SHARDS // group)(lambda g: some(g, 0))

        @each(0, QB, 4)
        def _(b):
            sent[b] = run[chains[LAST_SRC, b]].astype(BF16)

    back(c_ea, ret_a, run_sa, s_fa)
    start_all(c_dfa, HEADS)
    o_fa = pltpu.make_async_copy(s_fa.at[h], r_fa.at[h], out.at[1])
    o_fa.start()
    back(c_eb, ret_b, run_sb, s_fb)
    start_all(c_dfb, HEADS)
    o_fb = pltpu.make_async_copy(s_fb.at[h], r_fb.at[h], out.at[5])
    o_fb.start()
    recv_all(c_x, NX)
    wz_p[...] = wx_r[0] + wx_r[1] + wx_r[2] + wx_r[3]
    wz_r[z] = wz_p[z]
    start_all(c_z, NZ)

    recv_all(c_a, HEADS)
    o_q = pltpu.make_async_copy(r_a.at[:, pl.ds(HS, HS)], q_out, out.at[3])
    o_q.start()
    recv_all(c_m, HEADS)
    per = HEADS // 2
    acc = jnp.zeros((BLOCK, D), F32)
    for i in range(2):
        wide = jnp.concatenate([r_a[per * i + k, :HS] for k in range(per)], axis=0).T
        acc = acc + nn(wide, owv[half * i : half * (i + 1)])
    mixed = [
        jnp.concatenate([r_m[per * i + k] for k in range(per)], axis=0).T for i in range(2)
    ]
    lo_v[...] = (acc + jnp.concatenate(mixed, axis=1).astype(F32)).astype(BF16)
    o_lo = pltpu.make_async_copy(lo_v, lo_out, out.at[4])
    o_lo.start()
    recv_all(c_z, NZ)
    total = wz_r[0]
    for n in range(1, NZ):
        total = total + wz_r[n]
    wg_v[...] = total * (1.0 / math.sqrt(SHARDS * QB * BLOCK))
    o_wg = pltpu.make_async_copy(wg_v, wg_out, out.at[2])
    o_wg.start()

    for copy in (c_q, c_m, c_a, c_kv):
        send_all(copy, HEADS)
    for copy in (c_ea, c_eb):
        send_all(copy, SHARDS)
    send_all(c_x, NX)
    recv_all(c_kv, HEADS)
    recv_all(c_dfa, HEADS)
    recv_all(c_dfb, HEADS)
    for copy in (o_kv, o_fa, o_fb, o_wg, o_q, o_lo):
        copy.wait()

    for copy in (c_dfa, c_dfb):
        send_all(copy, HEADS)
    send_all(c_z, NZ)


def finish(
    lo, q, kv, fa, fb, wg, lo_out, gp_out, wg_out,
    lo_v, q_v, kv_v, fa_v, fb_v, wg_v, gp_v, sem,
):
    loads = [
        pltpu.make_async_copy(a, b, sem.at[n])
        for n, (a, b) in enumerate(
            ((lo, lo_v), (wg, wg_v), (q, q_v), (kv, kv_v), (fa, fa_v), (fb, fb_v))
        )
    ]
    for copy in loads:
        copy.start()
    stores = [
        pltpu.make_async_copy(a, b, sem.at[10 + n])
        for n, (a, b) in enumerate(((lo_v, lo_out), (wg_v, wg_out)))
    ]
    for copy in loads:
        copy.wait()
    for copy in stores:
        copy.start()
    wide = 8 * HS
    for i in range(HEADS // 2):
        rows = []
        for n in (2 * i, 2 * i + 1):
            rows += [q_v[n], kv_v[n], fa_v[n], fb_v[n]]
        lanes = pl.ds(wide * i, wide)
        gp_v[:, lanes] = jnp.concatenate(rows, axis=0).T
        if i % 2:
            lanes = pl.ds(wide * (i - 1), 2 * wide)
            stores.append(
                pltpu.make_async_copy(gp_v.at[:, lanes], gp_out.at[:, lanes], sem.at[6 + i // 2])
            )
            stores[-1].start()
    for copy in stores:
        copy.wait()


def body(
    projected, upstream, out_weight, tile_weights, tile_owner,
    source_block, target_block, key_blocks, key_count,
):
    any_space = pl.BlockSpec(memory_space=pl.ANY)

    def buf(*shape, dtype=BF16):
        return pltpu.VMEM(shape, dtype)

    def sems(n):
        return pltpu.SemaphoreType.DMA((n,))

    tiles = (HS, BLOCK)
    tall = jax.ShapeDtypeStruct((HEADS, *tiles), BF16)
    columns = D // SHARDS
    lo, q, kv, fa, fb, wg = pl.pallas_call(
        kernel,
        out_shape=(
            jax.ShapeDtypeStruct((BLOCK, D), BF16),
            tall,
            jax.ShapeDtypeStruct((HEADS, 2 * HS, BLOCK), BF16),
            jax.ShapeDtypeStruct((HEADS, MANY, BLOCK), BF16),
            jax.ShapeDtypeStruct((HEADS, FEW, BLOCK), BF16),
            jax.ShapeDtypeStruct((columns, HS), F32),
        ),
        in_specs=[any_space] * 9,
        out_specs=(any_space,) * 6,
        scratch_shapes=[
            buf(1, SHARDS * TILES, dtype=jnp.int32), pltpu.SMEM((SHARDS * TILES,), jnp.int32),
            pltpu.SMEM((SHARDS * TILES,), jnp.int32), pltpu.SMEM((KMAX, QB), jnp.int32),
            pltpu.SMEM((QB,), jnp.int32), buf(BLOCK, D), buf(columns, HS, dtype=F32),
            buf(SHARDS, BLOCK, dtype=jnp.int32), buf(2 * SHARDS, BLOCK, dtype=jnp.int32),
            pltpu.SMEM((2 * SHARDS, BLOCK), jnp.int32),
            buf(8, BLOCK, dtype=jnp.int32), pltpu.SMEM((8, BLOCK), jnp.int32),
            buf(BLOCK, 4 * D), buf(BLOCK, D), buf(D, D), buf(TILES, BLOCK, BLOCK),
            buf(HEADS, FEW, BLOCK), buf(HEADS, MANY, BLOCK), buf(HEADS, 3 * HS, BLOCK),
            buf(HEADS, FEW, BLOCK), buf(HEADS, MANY, BLOCK), buf(HEADS, 3 * HS, BLOCK),
            buf(QB, D, BLOCK), buf(QB, *tiles), buf(QB, BLOCK, 2 * HS),
            buf(TILES, FEW, BLOCK), buf(TILES, MANY, BLOCK),
            buf(SLOTS, FEW, BLOCK), buf(SLOTS, MANY, BLOCK),
            buf(SLOTS, FEW, BLOCK), buf(SLOTS, MANY, BLOCK),
            buf(SLOTS, MANY, BLOCK), buf(SLOTS, FEW, BLOCK),
            buf(SLOTS, MANY, BLOCK), buf(SLOTS, FEW, BLOCK),
            buf(SLOTS + 1, *tiles, dtype=F32), buf(SLOTS + 1, MANY, BLOCK, dtype=F32),
            buf(SLOTS + 1, FEW, BLOCK, dtype=F32),
            buf(QB * KMAX + 1, *tiles, dtype=F32), buf(QB * KMAX + 1, *tiles, dtype=F32),
            buf(HEADS, 2 * HS, BLOCK), buf(HEADS, 2 * HS, BLOCK),
            buf(HEADS, MANY, BLOCK), buf(HEADS, FEW, BLOCK), buf(HEADS, *tiles),
            buf(HEADS, 2 * HS, BLOCK), buf(HEADS, *tiles),
            buf(D, HS, dtype=F32), buf(SHARDS, D // SHARDS, HS, dtype=F32),
            buf(NX, NZ, D // SHARDS, HS, dtype=F32),
            buf(NZ, D // SHARDS, HS, dtype=F32), buf(NZ, D // SHARDS, HS, dtype=F32),
            sems(9), sems(2), sems(6), *[sems(HEADS)] * 6,
            sems(7), sems(7), sems(7), sems(7), sems(8), sems(8), *[sems(SHARDS)] * 8,
            *[sems(HEADS)] * 10, sems(NX), sems(NX), sems(NZ), sems(NZ),
        ],
        compiler_params=pltpu.CompilerParams(
            collective_id=0, has_side_effects=True, vmem_limit_bytes=61 << 20
        ),
    )(
        tile_owner.T, source_block, target_block, key_blocks.T, key_count,
        projected, upstream, out_weight, tile_weights,
    )
    layer_out, grad_projected, weight_grad = pl.pallas_call(
        finish,
        out_shape=(
            jax.ShapeDtypeStruct((BLOCK, D), BF16),
            jax.ShapeDtypeStruct((BLOCK, 4 * D), BF16),
            jax.ShapeDtypeStruct((columns, HS), F32),
        ),
        in_specs=[any_space] * 6,
        out_specs=(any_space,) * 3,
        scratch_shapes=[
            buf(BLOCK, D), buf(HEADS, *tiles), buf(HEADS, 2 * HS, BLOCK), buf(HEADS, MANY, BLOCK),
            buf(HEADS, FEW, BLOCK), buf(columns, HS, dtype=F32), buf(BLOCK, 4 * D), sems(12),
        ],
        compiler_params=pltpu.CompilerParams(vmem_limit_bytes=61 << 20),
    )(lo, q, kv, fa, fb, wg)
    return layer_out, grad_projected, weight_grad.T


def solution(mesh):
    in_specs = (
        P(("seq", "head"), None), P(("seq", "head"), None), P(), P("seq", None, None),
        P(), P(), P(), P("seq", None), P("seq"),
    )
    out_specs = (P(("seq", "head"), None), P(("seq", "head"), None), P("head", "seq"))
    return jax.shard_map(body, mesh=mesh, in_specs=in_specs, out_specs=out_specs, check_vma=False)
```
